32 devices in a mesh: rep: 8 (over y, x, core), shard: 4 (over z).
Axes of the slice: x: 2, y: 2, z: 4, core: 2. Of those that a mesh axis runs over, the one named last changes fastest.
Arguments:
- tokens: bfloat16 [4096, 768], P(('rep', 'shard')), may hold values from -6 to 6
- w_qkv: bfloat16 [768, 2304], P('shard'), may hold values from -0.21875 to 0.21875
- w_out: bfloat16 [768, 768], P('shard'), may hold values from -1.25 to 1.25
- w_up: bfloat16 [768, 3072], P('shard'), may hold values from -0.21875 to 0.21875
- w_down: bfloat16 [3072, 768], P('shard'), may hold values from -0.109375 to 0.109375
- vec_bias: bfloat16 [6, 768], P(None, 'shard'), may hold values from -1.796875 to 1.796875
- ln_gain: bfloat16 [2, 768], P(None, 'shard'), may hold values from 0.5 to 1.5
- hidden_bias: bfloat16 [3072], P('shard'), may hold values from -1.796875 to 1.796875
- seq_lengths: int32 [32, 3], P(('rep', 'shard')), may hold values from 0 to 128, as said below
- cotangent: bfloat16 [4096, 768], P(('rep', 'shard')), may hold values from -6 to 6
Outputs:
- activations: bfloat16 [4096, 768], P(('rep', 'shard'))
- grad_tokens: float32 [4096, 768], P(('rep', 'shard'))
- grad_w_qkv: float32 [768, 2304], P('shard')
- grad_w_out: float32 [768, 768], P('shard')
- grad_w_up: float32 [768, 3072], P('shard')
- grad_w_down: float32 [3072, 768], P('shard')
- grad_vec_bias: float32 [6, 768], P(None, 'shard')
- grad_ln_gain: float32 [2, 768], P(None, 'shard')
- grad_hidden_bias: float32 [3072], P('shard')
The draws below stay inside these ranges and needn't reach their ends.
Inputs may be any that keep to these rules, and one draw needn't show every extreme that they name: `seq_lengths`: row r holds the lengths of the sequences packed into device r's rows, zeros last; each row sums to at most 128; at least two are nonzero except on one device, which holds a single sequence of exactly 128.
All inputs are finite; a program needn't handle non-finite values.
Results may differ from the reference program's by a relative error of at most 0.012.
Values may be sent and summed in bfloat16 or wider, within the bound.
No kernel may reach another device: no remote copies, remote signals or barrier semaphores. Data moves between devices by JAX's collectives and lax.ppermute only.
A program may use at most 128 MiB of HBM per device.

```python
import math
import jax
import jax.numpy as jnp
from jax import lax

D = 768
HEADS = 12
HEAD_DIM = 64
FF = 3072
TOK_DEV = 128
SLOTS = 3
RANKS = 32
TOKENS = 4096


def draw_seq_lengths(key, part):
    key = jax.random.fold_in(key, 7)
    key_count, key_len, key_full = jax.random.split(key, 3)
    counts = jax.random.randint(key_count, (RANKS,), 2, SLOTS + 1)
    lengths = jax.random.randint(key_len, (RANKS, SLOTS), TOK_DEV // 8, TOK_DEV // SLOTS + 1)
    slot_index = jnp.arange(SLOTS, dtype=jnp.int32)
    lengths = jnp.where(slot_index[None, :] < counts[:, None], lengths, 0)
    full_rank = jax.random.randint(key_full, (), 0, RANKS)
    full_row = jnp.where(slot_index == 0, TOK_DEV, 0)
    rank_index = jnp.arange(RANKS, dtype=jnp.int32)
    lengths = jnp.where(rank_index[:, None] == full_rank, full_row[None, :], lengths)
    return lengths.astype(jnp.int32)


def shard_levels(stream_key, dims, cuts, low, high):
    gain = 1.0
    for dim, shards_of in cuts:
        steps = jax.random.uniform(jax.random.fold_in(jax.random.fold_in(stream_key, 6), dim), (shards_of,), jnp.float32, low / len(cuts), high / len(cuts))
        gain = gain * jnp.repeat(jnp.exp(steps), dims[dim] // shards_of).reshape((-1,) + (1,) * (len(dims) - 1 - dim))
    return gain


def gaussian(rng, shape, deviation, most, cuts=(), kind=jnp.bfloat16):
    drawn = jax.random.normal(rng, shape, jnp.float32) * deviation
    if len(cuts) > 0:
        drawn = shard_levels(rng, shape, cuts, -0.22, 0.18) * drawn
    return jnp.clip(drawn, min=-most, max=most).astype(kind)


def setup_inputs(seed: int = 0) -> dict:
    arg_keys = jax.random.split(jax.random.key(seed), 11)
    tokens = gaussian(arg_keys[0], (TOKENS, D), 1.0, 6.0, ((0, 32),))
    w_qkv = gaussian(arg_keys[1], (D, 3 * D), D ** -0.5, 0.21875, ((0, 4),))
    w_out = gaussian(arg_keys[2], (D, D), (D // 32) ** -0.5, 1.25, ((0, 4),))
    w_up = gaussian(arg_keys[3], (D, FF), D ** -0.5, 0.21875, ((0, 4),))
    w_down = gaussian(arg_keys[4], (FF, D), FF ** -0.5, 0.109375, ((0, 4),))
    vec_bias = gaussian(arg_keys[5], (6, D), 0.3, 1.796875, ((1, 4),))
    ln_gain = jnp.clip(1.0 + 0.1 * jax.random.normal(arg_keys[6], (2, D), jnp.float32), 0.5, 1.5).astype(jnp.bfloat16)
    hidden_bias = gaussian(arg_keys[7], (FF,), 0.3, 1.796875, ((0, 4),))
    seq_lengths = draw_seq_lengths(jax.random.fold_in(arg_keys[10], 71), 0)
    cotangent = gaussian(arg_keys[9], (TOKENS, D), 1.0, 6.0, ((0, 32),))
    return dict(tokens=tokens, w_qkv=w_qkv, w_out=w_out, w_up=w_up, w_down=w_down, vec_bias=vec_bias, ln_gain=ln_gain, hidden_bias=hidden_bias, seq_lengths=seq_lengths, cotangent=cotangent)


@jax.custom_vjp
def low(v):
    return lax.optimization_barrier(v.astype(jnp.bfloat16)).astype(jnp.float32)

@jax.custom_vjp
def low_back(v):
    return v

def low_keep(v):
    return (low(v), None)

def low_pass(kept, grad):
    return (grad,)

def back_keep(v):
    return (v, None)

def back_low(kept, grad):
    return (low(grad),)
low.defvjp(low_keep, low_pass)
low_back.defvjp(back_keep, back_low)
layer_eps = 1e-12
masked_score = -1000000000.0

def matmul_high(left_op, right_op):
    return jnp.dot(left_op, right_op, precision=lax.Precision.HIGHEST, preferred_element_type=jnp.float32)

def norm_rows(hidden, scale_row, shift_row):
    centre = hidden - lax.optimization_barrier(jnp.mean(hidden, axis=-1, keepdims=True))
    spread = lax.optimization_barrier(jnp.mean(centre * centre, axis=-1, keepdims=True))
    return centre * lax.rsqrt(spread + layer_eps) * scale_row + shift_row

def segment_ids(lengths, row_count):
    seq_ends = jnp.cumsum(lengths).astype(jnp.int32)
    position = jnp.arange(row_count, dtype=jnp.int32)
    segment = lax.optimization_barrier(jnp.sum((position[:, None] >= seq_ends[None, :]).astype(jnp.int32), axis=1))
    return (segment, position < seq_ends[-1])

def layer_block(params, inputs, lengths):
    w_qkv, w_out, w_up, w_down, vec_bias, ln_gain, hidden_bias = params
    blocks = lengths.shape[0]
    feat_width = inputs.shape[1]
    segment, row_valid = jax.vmap(lambda len_row: segment_ids(len_row, TOK_DEV))(lengths)
    zero_bias = jnp.zeros((feat_width,), jnp.float32)
    projected = matmul_high(inputs, w_qkv) + jnp.concatenate([vec_bias[0], zero_bias, vec_bias[1]])
    projected = low_back(low(projected)).reshape(blocks, TOK_DEV, 3, HEADS, HEAD_DIM)
    queries = projected[:, :, 0]
    key_rows = projected[:, :, 1]
    value_rows = projected[:, :, 2]
    scores = jnp.einsum('bqhd,bkhd->bhqk', queries, key_rows, precision=lax.Precision.HIGHEST) * (1.0 / math.sqrt(HEAD_DIM))
    same_seq = (segment[:, :, None] == segment[:, None, :])[:, None]
    scores = low_back(jnp.where(same_seq, scores, masked_score))
    row_top = lax.optimization_barrier(jnp.max(scores, axis=-1, keepdims=True))
    exp_terms = jnp.exp(scores - row_top)
    attn_probs = low(exp_terms / lax.optimization_barrier(jnp.sum(exp_terms, axis=-1, keepdims=True)))
    attn_mix = jnp.einsum('bhqk,bkhd->bqhd', attn_probs, value_rows, precision=lax.Precision.HIGHEST)
    attn_mix = low_back(low(attn_mix.reshape(blocks * TOK_DEV, feat_width)))
    attended = low_back(matmul_high(attn_mix, w_out) + vec_bias[2])
    normed_one = norm_rows(inputs + attended, ln_gain[0], vec_bias[3])
    hidden = low_back(matmul_high(low(normed_one), w_up) + hidden_bias)
    active = low(jax.nn.gelu(hidden, approximate=False))
    branch = low_back(matmul_high(active, w_down) + vec_bias[4])
    result = norm_rows(normed_one + branch, ln_gain[1], vec_bias[5])
    return result * row_valid.reshape(-1, 1).astype(jnp.float32)

def reference(tokens, w_qkv, w_out, w_up, w_down, vec_bias, ln_gain, hidden_bias, seq_lengths, cotangent):
    params = tuple((argument.astype(jnp.float32) for argument in (w_qkv, w_out, w_up, w_down, vec_bias, ln_gain, hidden_bias)))
    group_size = math.gcd(RANKS, max(1, 4096 // TOK_DEV))
    steps_count = RANKS // group_size
    inputs = tokens.astype(jnp.float32).reshape(steps_count, group_size * TOK_DEV, D)
    lengths = seq_lengths.reshape(steps_count, group_size, SLOTS)

    def forward(param_set, rows_in):
        block_fn = jax.checkpoint(lambda rows_blk, len_blk: layer_block(param_set, rows_blk, len_blk))
        return lax.map(lambda pair_in: block_fn(pair_in[0], pair_in[1]), (rows_in, lengths))
    outputs, pull_back = jax.vjp(forward, params, inputs)
    param_grads, input_grad = pull_back(cotangent.astype(jnp.float32).reshape(outputs.shape))
    activations = outputs.reshape(TOKENS, D).astype(jnp.bfloat16)
    return (activations, input_grad.reshape(TOKENS, D), param_grads[0], param_grads[1], param_grads[2], param_grads[3], param_grads[4], param_grads[5], param_grads[6])
```

```python
import math

import jax
import jax.numpy as jnp
from jax import lax
from jax.sharding import PartitionSpec as P

HEADS = 12
HEAD_DIM = 64
PARTS = 4
CORES = 2
layer_eps = 1e-12
masked_score = -1000000000.0
BF = jnp.bfloat16
F32 = jnp.float32


def mm(a, b):
    return jnp.dot(a, b, preferred_element_type=F32)


def mm_ta(a, b):
    return lax.dot_general(a, b, (((0,), (0,)), ((), ())), preferred_element_type=F32)


def mm_tb(a, b):
    return lax.dot_general(a, b, (((1,), (1,)), ((), ())), preferred_element_type=F32)


def norm_stats(h):
    centre = h - jnp.mean(h, axis=-1, keepdims=True)
    inv = lax.rsqrt(jnp.mean(centre * centre, axis=-1, keepdims=True) + layer_eps)
    return centre * inv, inv


def norm_back(g, unit, inv, gain):
    gg = g * gain
    m1 = jnp.mean(gg, axis=-1, keepdims=True)
    m2 = jnp.mean(gg * unit, axis=-1, keepdims=True)
    return inv * (gg - m1 - unit * m2)


def gelu_parts(u):
    phi = 0.5 * (1.0 + lax.erf(u * (1.0 / math.sqrt(2.0))))
    dens = jnp.exp(-0.5 * u * u) * (1.0 / math.sqrt(2.0 * math.pi))
    return phi, phi + u * dens


def rows_of(flat, start, size):
    return lax.dynamic_slice_in_dim(flat, start, size, 0)


def make_body(reps, shards):
    def xor_perm(n, k):
        return [(i, i ^ k) for i in range(n)]

    def swap_core(v):
        return lax.ppermute(v, "rep", xor_perm(reps, 1))

    def swap_part(v, k):
        return lax.ppermute(v, "rep", xor_perm(reps, CORES * k))

    def swap_shard(v, k):
        return lax.ppermute(v, "shard", xor_perm(shards, k))

    def spread_part(v):
        return [v] + [swap_part(v, k) for k in range(1, PARTS)]

    def spread_shard(v):
        return [v] + [swap_shard(v, k) for k in range(1, shards)]

    def in_order(slots, me):
        stacked = jnp.stack(slots)
        return jnp.stack(
            [lax.dynamic_index_in_dim(stacked, j ^ me, 0, False) for j in range(len(slots))]
        )

    def pick(stacked, index):
        return lax.dynamic_index_in_dim(stacked, index, 0, False)

    def pair(mine, other, core):
        first = core == 0
        return jnp.where(first, mine, other), jnp.where(first, other, mine)

    def sum_outer(v):
        step = CORES * PARTS
        while step < reps:
            got = lax.ppermute(v, "rep", xor_perm(reps, step))
            v = v + got
            step *= 2
        return v

    def body(
        tokens, w_qkv, w_out, w_up, w_down, vec_bias, ln_gain, hidden_bias, seq_lengths, cotangent
    ):
        rows, width = tokens.shape
        hidden = hidden_bias.shape[0] * shards
        wsh = width // shards
        half = wsh // CORES
        hcol = width // PARTS
        fcol = hidden // shards // PARTS
        heads = HEADS // PARTS
        oq = wsh // PARTS // CORES
        rep = lax.axis_index("rep")
        z = lax.axis_index("shard")
        core = rep % CORES
        c = (rep // CORES) % PARTS

        len_row = jnp.pad(seq_lengths.astype(BF), ((0, 15), (0, width - seq_lengths.shape[1])))
        tok_slots = spread_part(jnp.concatenate([tokens, len_row]))

        qkv_c = lax.dynamic_index_in_dim(
            w_qkv.reshape(wsh, 3, PARTS, hcol), c, 2, False
        ).reshape(wsh, 3 * hcol)
        extra = jnp.concatenate(
            [vec_bias, ln_gain, lax.dynamic_slice_in_dim(hidden_bias, c * fcol, fcol)[None]]
        ).reshape(3, 3 * hcol)
        extra = jnp.pad(extra, ((0, 13), (0, 0)))
        pay1 = jnp.concatenate([rows_of(qkv_c, core * half, half), extra])
        got1 = in_order(spread_shard(pay1), z)
        ext = got1[:, half : half + 3].reshape(shards, 9, hcol)
        q_lo, q_hi = pair(got1[:, :half], swap_core(got1[:, :half]), core)
        wq = jnp.concatenate([q_lo, q_hi], axis=1).reshape(width, 3 * hcol)
        vecs = ext[:, :6].transpose(1, 0, 2).reshape(6, width).astype(F32)
        gains = ext[:, 6:8].transpose(1, 0, 2).reshape(2, width).astype(F32)
        hid_b = ext[:, 8].reshape(1, shards * fcol).astype(F32)

        out_q = rows_of(w_out, c * (wsh // PARTS) + core * oq, oq)
        got_o = jnp.stack(spread_shard(out_q))
        up_c = lax.dynamic_index_in_dim(
            w_up.reshape(wsh, shards, PARTS, fcol), c, 2, False
        ).reshape(wsh, shards * fcol)
        down_c = rows_of(w_down, c * fcol, fcol)
        pay2 = jnp.concatenate(
            [rows_of(up_c, core * half, half), rows_of(down_c, core * (fcol // 2), fcol // 2)]
        )
        got2 = in_order(spread_shard(pay2), z)
        lo2, hi2 = pair(got2, swap_core(got2), core)
        wu = jnp.concatenate([lo2[:, :half], hi2[:, :half]], axis=1).reshape(width, -1)
        wd = jnp.concatenate([lo2[:, half:], hi2[:, half:]], axis=1).reshape(-1, width)
        part_o = in_order(spread_part(in_order(list(got_o), z)), c)
        o_lo, o_hi = pair(part_o, swap_core(part_o), core)
        wo = jnp.stack([o_lo, o_hi], axis=2).transpose(1, 0, 2, 3, 4).reshape(width, width)

        xg = jnp.stack([s[:rows] for s in tok_slots])
        lens = jnp.stack([s[rows, : seq_lengths.shape[1]] for s in tok_slots]).astype(jnp.int32)
        ends = jnp.cumsum(lens, axis=1)
        pos = jnp.arange(rows, dtype=jnp.int32)
        seg = jnp.sum((pos[None, :, None] >= ends[:, None, :]).astype(jnp.int32), axis=2)
        same = seg[:, :, None] == seg[:, None, :]
        keep = (pos < ends[0, -1]).astype(F32)[:, None]
        xf = xg.reshape(PARTS * rows, width)
        qb = jnp.concatenate(
            [
                lax.dynamic_slice_in_dim(vecs[0], c * hcol, hcol),
                jnp.zeros((hcol,), F32),
                lax.dynamic_slice_in_dim(vecs[1], c * hcol, hcol),
            ]
        )
        proj = (mm(xf, wq) + qb).astype(BF).reshape(PARTS, rows, 3, heads, HEAD_DIM)
        q, kk, v = proj[:, :, 0], proj[:, :, 1], proj[:, :, 2]
        scale = 1.0 / math.sqrt(HEAD_DIM)
        s = jnp.einsum("bqhd,bkhd->bhqk", q, kk, preferred_element_type=F32) * scale
        s = jnp.where(same[:, None], s, masked_score)
        top = jnp.max(s, axis=-1, keepdims=True)
        e = jnp.exp(s - top)
        probs = e / jnp.sum(e, axis=-1, keepdims=True)
        probs_low = probs.astype(BF)
        mix = jnp.einsum("bhqk,bkhd->bqhd", probs_low, v, preferred_element_type=F32)
        mix = mix.astype(BF).reshape(PARTS, rows, hcol)
        mix_slots = [mix[0]] + [swap_part(mix[k], k) for k in range(1, PARTS)]
        mix_full = in_order(mix_slots, c).transpose(1, 0, 2).reshape(rows, width)

        h1 = tokens.astype(F32) + (mm(mix_full, wo) + vecs[2])
        unit1, inv1 = norm_stats(h1)
        y1 = unit1 * gains[0] + vecs[3]
        y1_low = y1.astype(BF)
        yg = jnp.stack(spread_part(y1_low)).reshape(PARTS * rows, width)

        u = mm(yg, wu) + hid_b
        phi, slope = gelu_parts(u)
        act = (u * phi).astype(BF)
        zp = mm(act, wd).reshape(PARTS, rows, width)
        branch = zp[0] + vecs[4]
        for k in range(1, PARTS):
            branch = branch + swap_part(zp[k].astype(BF), k).astype(F32)

        unit2, inv2 = norm_stats(y1 + branch)
        activations = ((unit2 * gains[1] + vecs[5]) * keep).astype(BF)
        g_res = cotangent.astype(F32) * keep
        g_gain2 = jnp.sum(g_res * unit2, axis=0)
        g_shift2 = jnp.sum(g_res, axis=0)
        g_h2 = norm_back(g_res, unit2, inv2, gains[1])
        dz = g_h2.astype(BF)
        g_bias4 = jnp.sum(dz.astype(F32), axis=0)
        dzg = jnp.stack(spread_part(dz)).reshape(PARTS * rows, width)

        du = (mm_tb(dzg, wd) * slope).astype(BF)
        g_hid = jnp.sum(du.astype(F32), axis=0)
        dyp = mm_tb(du, wu).reshape(PARTS, rows, width)
        dy1 = g_h2 + dyp[0]
        for k in range(1, PARTS):
            dy1 = dy1 + swap_part(dyp[k].astype(BF), k).astype(F32)
        g_down = mm_ta(act, dzg).astype(BF)
        g_up = mm_ta(yg, du).astype(BF)

        hid_rows = jnp.pad(
            g_hid.astype(BF).reshape(shards, 1, 1, fcol), ((0, 0), (0, 1), (0, 15), (0, width - fcol))
        )
        hid_rows = jnp.concatenate([hid_rows[:, :1], hid_rows[:, :1]], axis=1)
        batch1 = jnp.concatenate(
            [
                g_up.reshape(shards, CORES, half, width),
                g_down.reshape(shards, CORES, fcol // 2, width),
                hid_rows,
            ],
            axis=2,
        )

        def reduce_batch(batch):
            b = batch.transpose(1, 0, 2, 3)
            mine, give = pick(b, core), pick(b, 1 - core)
            tot = mine.astype(F32) + swap_core(give).astype(F32)
            low = tot.astype(BF)
            own = pick(tot, z)
            for k in range(1, shards):
                own = own + swap_shard(pick(low, z ^ k), k).astype(F32)
            return sum_outer(own)

        def spread_batch(piece):
            full = in_order(spread_part(piece.astype(BF)), c)
            lo, hi = pair(full, swap_core(full), core)
            return jnp.stack([lo, hi], axis=1)

        done1 = spread_batch(reduce_batch(batch1))
        gw_up = (
            done1[:, :, :half]
            .reshape(PARTS, CORES, half, shards, fcol)
            .transpose(1, 2, 3, 0, 4)
            .reshape(wsh, hidden)
            .astype(F32)
        )
        gw_down = done1[:, :, half : half + fcol // 2].reshape(PARTS * fcol, width).astype(F32)
        g_hidden = done1[:, 0, half + fcol // 2, :fcol].reshape(-1).astype(F32)

        g_gain1 = jnp.sum(dy1 * unit1, axis=0)
        g_shift1 = jnp.sum(dy1, axis=0)
        g_h1 = norm_back(dy1, unit1, inv1, gains[0])
        da = g_h1.astype(BF)
        g_bias2 = jnp.sum(da.astype(F32), axis=0)
        dmix = mm_tb(da, wo).astype(BF).reshape(rows, PARTS, hcol).transpose(1, 0, 2)
        dm_slots = [pick(dmix, c)] + [swap_part(pick(dmix, c ^ k), k) for k in range(1, PARTS)]
        dm = jnp.stack(dm_slots).reshape(PARTS, rows, heads, HEAD_DIM)
        g_out = mm_ta(mix_full, da).astype(BF).reshape(shards, PARTS, CORES, oq, width)
        go = g_out.transpose(2, 1, 0, 3, 4)
        go = pick(go, core).astype(F32) + swap_core(pick(go, 1 - core)).astype(F32)
        go_low = go.astype(BF)
        go_sum = pick(go, c)
        for k in range(1, PARTS):
            go_sum = go_sum + swap_part(pick(go_low, c ^ k), k).astype(F32)

        dv = jnp.einsum("bhqk,bqhd->bkhd", probs_low, dm, preferred_element_type=F32)
        dpr = jnp.einsum("bqhd,bkhd->bhqk", dm, v, preferred_element_type=F32)
        inner = jnp.sum(probs * dpr, axis=-1, keepdims=True)
        ds = (probs * (dpr - inner)).astype(BF)
        dq = jnp.einsum("bhqk,bkhd->bqhd", ds, kk, preferred_element_type=F32) * scale
        dk = jnp.einsum("bhqk,bqhd->bkhd", ds, q, preferred_element_type=F32) * scale
        dp = (
            jnp.stack([dq, dk, dv], axis=2).astype(BF).reshape(PARTS * rows, 3 * hcol)
        )
        g_qkv = mm_ta(xf, dp).astype(BF)
        dxp = mm_tb(dp, wq).reshape(PARTS, rows, width)
        g_tok = g_h1 + dxp[0]
        for k in range(1, PARTS):
            g_tok = g_tok + swap_part(dxp[k].astype(BF), k).astype(F32)

        col = jnp.sum(dp.astype(F32), axis=0)
        qv = jnp.stack([col[:hcol], col[2 * hcol :]]).astype(BF)
        small = jnp.stack([g_bias2, g_shift1, g_bias4, g_shift2, g_gain1, g_gain2]).astype(BF)
        small = small.reshape(6, shards, wsh).transpose(1, 0, 2)
        at_c = (jnp.arange(shards) == c)[:, None, None]
        qv = jnp.where(at_c, qv[None], jnp.zeros((), BF))
        small = jnp.concatenate([qv, small], axis=1).reshape(shards, 1, -1)
        span = 3 * hcol
        extra_rows = -(-(8 * wsh) // span)
        small = jnp.pad(small, ((0, 0), (0, 0), (0, extra_rows * span - 8 * wsh)))
        small = small.reshape(shards, extra_rows, span)
        small = jnp.broadcast_to(small[:, None], (shards, CORES, extra_rows, span))
        batch2 = jnp.concatenate([g_qkv.reshape(shards, CORES, half, span), small], axis=2)
        piece2 = reduce_batch(batch2)
        own_o = pick(go_sum, z)
        go_sum_low = go_sum.astype(BF)
        for k in range(1, shards):
            own_o = own_o + swap_shard(pick(go_sum_low, z ^ k), k).astype(F32)
        own_o = sum_outer(own_o)
        done2 = spread_batch(piece2)
        done_o = spread_batch(own_o)
        gw_qkv = (
            done2[:, :, :half]
            .reshape(PARTS, CORES, half, 3, hcol)
            .transpose(1, 2, 3, 0, 4)
            .reshape(wsh, 3 * width)
            .astype(F32)
        )
        gw_out = done_o.reshape(wsh, width).astype(F32)
        tot_small = jnp.sum(done2[:, 0, half:].astype(F32), axis=0).reshape(-1)[: 8 * wsh]
        tot_small = tot_small.reshape(8, wsh)
        return (
            activations,
            g_tok,
            gw_qkv,
            gw_out,
            gw_up,
            gw_down,
            tot_small[:6],
            tot_small[6:],
            g_hidden,
        )

    return body


def solution(mesh):
    body = make_body(mesh.shape["rep"], mesh.shape["shard"])
    both = P(("rep", "shard"), None)
    first = P("shard", None)
    return jax.shard_map(
        body,
        mesh=mesh,
        in_specs=(
            both,
            first,
            first,
            first,
            first,
            P(None, "shard"),
            P(None, "shard"),
            P("shard"),
            both,
            both,
        ),
        out_specs=(
            both,
            both,
            first,
            first,
            first,
            first,
            P(None, "shard"),
            P(None, "shard"),
            P("shard"),
        ),
        check_vma=False,
    )
```

```python
import functools
import math

import jax
import jax.numpy as jnp
from jax import lax
from jax.experimental import pallas as pl
from jax.experimental.pallas import tpu as pltpu
from jax.sharding import PartitionSpec as P

HEADS = 12
HEAD_DIM = 64
PARTS = 4
CORES = 2
layer_eps = 1e-12
masked_score = -1000000000.0
BF = jnp.bfloat16
F32 = jnp.float32
VMEM_BYTES = 48 * 1024 * 1024
PACK_BYTES = 62 * 1024 * 1024
COST = 11 * 10**9


def mm(a, b):
    return jnp.dot(a, b, preferred_element_type=F32)


def mm_ta(a, b):
    return lax.dot_general(a, b, (((0,), (0,)), ((), ())), preferred_element_type=F32)


def mm_tb(a, b):
    return lax.dot_general(a, b, (((1,), (1,)), ((), ())), preferred_element_type=F32)


def at(start, size, unit):
    return pl.ds(pl.multiple_of(start, unit), size)


def norm_stats(h):
    centre = h - jnp.mean(h, axis=-1, keepdims=True)
    inv = lax.rsqrt(jnp.mean(centre * centre, axis=-1, keepdims=True) + layer_eps)
    return centre * inv, inv


def norm_back(g, unit, inv, gain):
    gg = g * gain
    m1 = jnp.mean(gg, axis=-1, keepdims=True)
    m2 = jnp.mean(gg * unit, axis=-1, keepdims=True)
    return inv * (gg - m1 - unit * m2)


def gelu_parts(u):
    phi = 0.5 * (1.0 + lax.erf(u * (1.0 / math.sqrt(2.0))))
    dens = jnp.exp(-0.5 * u * u) * (1.0 / math.sqrt(2.0 * math.pi))
    return phi, phi + u * dens


def col_sum(v):
    return jnp.sum(v, axis=0, keepdims=True)


def fold_piece(put, get, cols):
    put(0, 0, get(0, 0, cols))
    put(1, 0, get(1, 0, cols))
    put(0, cols, get(2, 0, cols // 2))
    put(1, cols, get(2, cols // 2, cols // 2))


def pack_kernel(idx, tok, wqkv, wout, vec_in, gain_in, hid_in, lens_in, xp, pay, bq, bo, vec, gain, hid, lens, sem):
    rows, width = tok.shape
    half = bq.shape[0]
    piece, ocol = bo.shape
    hc = width // PARTS
    fc = hid.shape[1] // PARTS
    load_q = pltpu.make_async_copy(wqkv.at[at(idx[1] * half, half, 32)], bq, sem.at[0])
    load_o = pltpu.make_async_copy(
        wout.at[at(idx[0] * piece, piece, 16), at(idx[1] * ocol, ocol, 128)], bo, sem.at[1]
    )
    load_x = pltpu.make_async_copy(tok, xp.at[:rows], sem.at[2])
    small = [
        pltpu.make_async_copy(a, b, sem.at[3 + n])
        for n, (a, b) in enumerate(
            ((vec_in, vec), (gain_in, gain), (hid_in, hid), (lens_in, lens))
        )
    ]
    load_q.start()
    load_x.start()
    load_o.start()
    for load in small:
        load.start()
    base = half + 16
    pay[half:base] = jnp.zeros((16, 3 * hc), BF)
    xp[rows:] = jnp.zeros((16, width), BF)
    for load in small:
        load.wait()
    xp[rows : rows + 1, : lens.shape[1]] = lens[...].astype(BF)
    for n in range(8):
        src = vec[n : n + 1, :] if n < 6 else gain[n - 6 : n - 5, :]
        pay[half + n // 3 : half + n // 3 + 1, (n % 3) * hc : (n % 3 + 1) * hc] = src
    load_o.wait()
    third = piece // 3

    def put(row, col, v):
        pay[base + row * third : base + (row + 1) * third, col : col + v.shape[1]] = v

    fold_piece(put, lambda g, col, n: bo[g * third : (g + 1) * third, col : col + n], ocol)
    load_q.wait()
    for j in range(PARTS):

        @pl.when(idx[0] == j)
        def _(j=j):
            pay[half + 2 : half + 3, 2 * hc :] = hid[:, j * fc : (j + 1) * fc]
            for s in range(3):
                pay[:half, s * hc : (s + 1) * hc] = bq[
                    :, s * width + j * hc : s * width + (j + 1) * hc
                ]

    load_x.wait()


def pack2_kernel(idx, wup, wdown, pay, bu, sem):
    half = bu.shape[0]
    fc = pay.shape[0] - half
    units = wdown.shape[0]
    shards = wup.shape[1] // units
    fpart = units // PARTS
    load_u = pltpu.make_async_copy(wup.at[at(idx[1] * half, half, 32)], bu, sem.at[0])
    load_d = pltpu.make_async_copy(
        wdown.at[at(idx[0] * fpart + idx[1] * fc, fc, 32)], pay.at[half:], sem.at[1]
    )
    load_u.start()
    load_d.start()
    load_u.wait()
    for j in range(PARTS):

        @pl.when(idx[0] == j)
        def _(j=j):
            for s in range(shards):
                base = (s * PARTS + j) * fpart
                pay[:half, s * fpart : (s + 1) * fpart] = bu[:, base : base + fpart]

    load_d.wait()


def split_kernel(g0, g1, g2, g3, first, second):
    base = first.shape[1]
    for k, g in enumerate((g0, g1, g2, g3)):
        first[k] = g[:base, :]
        cols = second.shape[2]
        third = second.shape[1] // 3
        top, low = g[base : base + third, :], g[base + third :, :]
        second[k, :third] = top[:, :cols]
        second[k, third : 2 * third] = low[:, :cols]
        second[k, 2 * third :, : cols // 2] = top[:, cols:]
        second[k, 2 * third :, cols // 2 :] = low[:, cols:]


def sum_kernel(own, got, out):
    out[...] = (own[...] + got[...].astype(F32)).astype(out.dtype)


def wq_kernel(idx, mine, other, wq, small, bias):
    c, core, z = idx[0], idx[1], idx[2]
    shards, _, span = mine.shape
    hc = span // 3
    half = wq.shape[0] // shards // CORES
    for m in range(shards):
        base = (z ^ m) * (CORES * half)
        wq[at(base + core * half, half, 32), :] = mine[m, :half, :]
        wq[at(base + (1 - core) * half, half, 32), :] = other[m, :half, :]
    small[...] = jnp.zeros_like(small)
    for j in range(shards):
        e = mine[j ^ z, half:, :].astype(F32)
        for n in range(9):
            small[n : n + 1, j * hc : (j + 1) * hc] = e[
                n // 3 : n // 3 + 1, (n % 3) * hc : (n % 3 + 1) * hc
            ]
    e = mine[c ^ z, half:, :].astype(F32)[:1]
    row = jnp.concatenate([e[:, :hc], jnp.zeros((1, hc), F32), e[:, hc : 2 * hc]], axis=1)
    bias[...] = jnp.broadcast_to(row, bias.shape)


def attn_kernel(x, wq, bias, pj, probs, out):
    rows, span = pj.shape
    hc = span // 3
    heads = hc // HEAD_DIM
    scale = 1.0 / math.sqrt(HEAD_DIM)
    pj[...] = (mm(x[:rows, :], wq[...]) + bias[:1, :]).astype(BF)
    pos_r = lax.broadcasted_iota(jnp.int32, (rows, 1), 0).astype(F32)
    pos_c = lax.broadcasted_iota(jnp.int32, (1, rows), 1).astype(F32)
    lens = x[rows : rows + 16, :128].astype(F32)[:1]
    end = jnp.zeros((1, 1), F32)
    seg_r = jnp.zeros((rows, 1), F32)
    seg_c = jnp.zeros((1, rows), F32)
    for n in range(3):
        end = end + lens[:, n : n + 1]
        seg_r = seg_r + (pos_r >= end).astype(F32)
        seg_c = seg_c + (pos_c >= end).astype(F32)
    same = seg_r == seg_c
    pb = pj[...]
    mixes = []
    for h in range(heads):
        q = pb[:, h * HEAD_DIM : (h + 1) * HEAD_DIM]
        k = pb[:, hc + h * HEAD_DIM : hc + (h + 1) * HEAD_DIM]
        v = pb[:, 2 * hc + h * HEAD_DIM : 2 * hc + (h + 1) * HEAD_DIM]
        s = jnp.where(same, mm_tb(q, k) * scale, masked_score)
        e = jnp.exp(s - jnp.max(s, axis=-1, keepdims=True))
        p = e / jnp.sum(e, axis=-1, keepdims=True)
        probs[h] = p
        mixes.append(mm(p.astype(BF), v))
    out[...] = jnp.concatenate(mixes, axis=1).astype(BF)


def wo_kernel(idx, mine, other, wo):
    c, core, z = idx[0], idx[1], idx[2]
    parts, shards, piece, cols = mine.shape
    for k in range(parts):
        for m in range(shards):
            base = at((z ^ m) * (parts * piece) + (c ^ k) * piece, piece, 16)
            wo[base, at(core * cols, cols, 128)] = mine[k, m]
            wo[base, at((1 - core) * cols, cols, 128)] = other[k, m]


def out_kernel(idx, tok, m0, m1, m2, m3, wo, small, y1, y1low, unit, inv):
    c = idx[0]
    hc = m0.shape[1]
    acc = small[2:3, :]
    for k, m in enumerate((m0, m1, m2, m3)):
        acc = acc + mm(m[...], wo[at((c ^ k) * hc, hc, 64), :])
    u, r = norm_stats(tok[...].astype(F32) + acc)
    unit[...] = u
    inv[...] = jnp.broadcast_to(r, inv.shape)
    y = u * small[6:7, :] + small[3:4, :]
    y1[...] = y
    y1low[...] = y.astype(BF)


def join_kernel(g0, g1, g2, g3, out):
    for k, g in enumerate((g0, g1, g2, g3)):
        out[k] = g[...]


def w2_kernel(idx, mine, other, wu, wd):
    core, z = idx[1], idx[2]
    half = mine.shape[1] // 2
    for m in range(mine.shape[0]):
        base = (z ^ m) * (2 * half)
        lo = at(base + core * half, half, 32)
        hi = at(base + (1 - core) * half, half, 32)
        wu[lo, :] = mine[m, :half, :]
        wu[hi, :] = other[m, :half, :]
        wd[lo, :] = mine[m, half:, :]
        wd[hi, :] = other[m, half:, :]


def ffn_kernel(y, wu, wd, small, act, slope, out):
    u = mm(y[...], wu[...]) + small[8:9, :]
    phi, slp = gelu_parts(u)
    a = (u * phi).astype(BF)
    act[...] = a
    slope[...] = slp
    out[...] = mm(a, wd[...]).astype(out.dtype)


def ln2_kernel(y1, z0, r1, r2, r3, small, cot, x0, actv, dz, gh2, sm):
    rows = y1.shape[0]
    branch = z0[...] + r1[...].astype(F32) + r2[...].astype(F32) + r3[...].astype(F32)
    u, r = norm_stats(y1[...] + (branch + small[4:5, :]))
    lens = x0[rows : rows + 16, :128].astype(F32)[:1]
    total = lens[:, 0:1] + lens[:, 1:2] + lens[:, 2:3]
    keep = (lax.broadcasted_iota(jnp.int32, (rows, 1), 0).astype(F32) < total).astype(F32)
    actv[...] = ((u * small[7:8, :] + small[5:6, :]) * keep).astype(BF)
    g = cot[...].astype(F32) * keep
    gh = norm_back(g, u, r, small[7:8, :])
    gh2[...] = gh
    low = gh.astype(BF)
    dz[...] = low
    sm[...] = jnp.zeros_like(sm)
    sm[0:1, :] = col_sum(low.astype(F32))
    sm[1:2, :] = col_sum(g)
    sm[2:3, :] = col_sum(g * u)


def ffb_kernel(d, wu, wd, slope, du, out):
    t = (mm_tb(d[...], wd[...]) * slope[...]).astype(BF)
    du[...] = t
    out[...] = mm_tb(t, wu[...]).astype(out.dtype)


def ffw_kernel(idx, *refs):
    core = idx[1]
    groups = [refs[n * PARTS : (n + 1) * PARTS] for n in range(4)]
    give, mine, hid, left, right, full = refs[4 * PARTS :]
    rows, width = groups[0][0].shape
    shards = give.shape[0]
    half = width // shards // CORES
    acts, dzs, ys, dus = groups
    h = None
    for base, lefts, rights in ((0, ys, dus), (half, acts, dzs)):
        for k in range(PARTS):
            left[k * rows : (k + 1) * rows, :] = lefts[k][...]
            right[k * rows : (k + 1) * rows, :] = rights[k][...]
        if base == 0:
            h = col_sum(right[...].astype(F32))
        full[...] = mm_ta(left[...], right[...]).astype(BF)
        for j in range(shards):
            mine[j, base : base + half, :] = full[at(j * 2 * half + core * half, half, 32), :]
            give[j, base : base + half, :] = full[
                at(j * 2 * half + (1 - core) * half, half, 32), :
            ]
    hid[...] = jnp.broadcast_to(h, hid.shape)


def add_kernel(idx, mine, got, keep, send):
    z = idx[2]
    for n in range(4):
        out, m, j = (keep, send)[n % 2], n // 2, z ^ n
        out[m] = (mine[j].astype(F32) + got[j].astype(F32)).astype(out.dtype)


def add_far_kernel(keep, got, own, send):
    own[...] = keep[0] + got[0].astype(F32)
    send[...] = (keep[1] + got[1].astype(F32)).astype(BF)


def fin1_kernel(idx, mine, other, gup, gdown):
    c, core = idx[0], idx[1]
    parts, _, width = mine.shape
    half = gup.shape[0] // 2
    fc = gdown.shape[0] // parts
    shards = gup.shape[1] // (parts * fc)
    for j in range(parts):
        k = j ^ c
        for src, row in ((mine, core * half), (other, (1 - core) * half)):
            v = src[k, :half, :].astype(F32)
            for s in range(shards):
                base = (s * parts + j) * fc
                gup[at(row, half, 32), base : base + fc] = v[:, s * fc : (s + 1) * fc]
            gdown[at(j * fc + row, half, 32), :] = src[k, half : 2 * half, :].astype(F32)


def ln1b_kernel(idx, gh2, o0, r1, r2, r3, unit, inv, small, wo, gh1, da, m0, m1, m2, m3, sm):
    c = idx[0]
    hc = m0.shape[1]
    dy = gh2[...] + o0[...] + r1[...].astype(F32) + r2[...].astype(F32) + r3[...].astype(F32)
    u = unit[...]
    gh = norm_back(dy, u, inv[:, :1], small[6:7, :])
    gh1[...] = gh
    low = gh.astype(BF)
    da[...] = low
    for k, m in enumerate((m0, m1, m2, m3)):
        m[...] = mm_tb(low, wo[at((c ^ k) * hc, hc, 64), :]).astype(BF)
    sm[...] = jnp.zeros_like(sm)
    sm[0:1, :] = col_sum(low.astype(F32))
    sm[1:2, :] = col_sum(dy)
    sm[2:3, :] = col_sum(dy * u)


def outw_kernel(idx, m0, m1, m2, m3, da, give, mine):
    c, core = idx[0], idx[1]
    cols = give.shape[2]
    lo, hi = da[:, :cols], da[:, cols:]
    first = core == 0
    keep = jnp.where(first, lo.astype(F32), hi.astype(F32)).astype(BF)
    pass_on = jnp.where(first, hi.astype(F32), lo.astype(F32)).astype(BF)
    for k, m in enumerate((m0, m1, m2, m3)):
        mine[c ^ k] = mm_ta(m[...], keep).astype(BF)
        give[c ^ k] = mm_ta(m[...], pass_on).astype(BF)


def oadd_kernel(idx, mine, got, own, s1, s2, s3):
    c = idx[0]
    shards, piece = own.shape[0], own.shape[1]
    for k, out in enumerate((own, s1, s2, s3)):
        rng = at((c ^ k) * piece, piece, 16)
        for j in range(shards):
            v = mine[j, rng, :].astype(F32) + got[j, rng, :].astype(F32)
            out[j] = v.astype(out.dtype)


def attb_kernel(d, pj, probs, dp):
    rows, hc = d.shape
    heads = hc // HEAD_DIM
    scale = 1.0 / math.sqrt(HEAD_DIM)
    pb = pj[...]
    db = d[...]
    dqs, dks, dvs = [], [], []
    for h in range(heads):
        q = pb[:, h * HEAD_DIM : (h + 1) * HEAD_DIM]
        k = pb[:, hc + h * HEAD_DIM : hc + (h + 1) * HEAD_DIM]
        v = pb[:, 2 * hc + h * HEAD_DIM : 2 * hc + (h + 1) * HEAD_DIM]
        g = db[:, h * HEAD_DIM : (h + 1) * HEAD_DIM]
        p = probs[h]
        dvs.append(mm_ta(p.astype(BF), g))
        dpr = mm_tb(g, v)
        inner = jnp.sum(p * dpr, axis=-1, keepdims=True)
        ds = (p * (dpr - inner)).astype(BF)
        dqs.append(mm(ds, k) * scale)
        dks.append(mm_ta(ds, q) * scale)
    dp[...] = jnp.concatenate(dqs + dks + dvs, axis=1).astype(BF)


def dx_kernel(d0, d1, d2, d3, wq, o0, o1, o2, o3):
    for d, out in ((d0, o0), (d1, o1), (d2, o2), (d3, o3)):
        out[...] = mm_tb(d[...], wq[...]).astype(out.dtype)


def qw_kernel(idx, x0, x1, x2, x3, d0, d1, d2, d3, sm1, sm2, hid, give, mine, xg, dp, full):
    c, core = idx[0], idx[1]
    shards, _, span = give.shape
    rows = d0.shape[0]
    hc = span // 3
    half = xg.shape[1] // shards // CORES
    for k, (x, d) in enumerate(((x0, d0), (x1, d1), (x2, d2), (x3, d3))):
        xg[k * rows : (k + 1) * rows, :] = x[:rows, :]
        dp[k * rows : (k + 1) * rows, :] = d[...]
    full[...] = mm_ta(xg[...], dp[...]).astype(BF)
    cols = col_sum(dp[...].astype(F32))
    vecs = (sm1[0:1], sm1[1:2], sm2[0:1], sm2[1:2], sm1[2:3], sm2[2:3])
    for j in range(shards):
        mine[j, :half, :] = full[at(j * 2 * half + core * half, half, 32), :]
        give[j, :half, :] = full[at(j * 2 * half + (1 - core) * half, half, 32), :]
        part = [v[:, j * hc : (j + 1) * hc] for v in vecs]
        own = jnp.where(c == j, 1.0, 0.0)
        rows = jnp.concatenate(
            [
                jnp.concatenate([cols[:, :hc] * own, cols[:, 2 * hc :] * own, part[0]], axis=1),
                jnp.concatenate(part[1:4], axis=1),
                jnp.concatenate(part[4:6] + [hid[:1, j * hc : (j + 1) * hc]], axis=1),
                jnp.zeros((13, span), F32),
            ],
            axis=0,
        ).astype(BF)
        mine[j, half:, :] = rows
        give[j, half:, :] = rows


def add2_kernel(idx, mine, got, osum, keep, send):
    z = idx[2]
    base, _ = mine.shape[1:]
    piece, cols = osum.shape[1:]
    third = piece // 3
    for n in range(4):
        out, m, j = (keep, send)[n % 2], n // 2, z ^ n
        out[m, :base, :] = (mine[j].astype(F32) + got[j].astype(F32)).astype(out.dtype)
        w = osum[j]

        def put(row, col, v, out=out, m=m):
            rng = slice(base + row * third, base + (row + 1) * third)
            out[m, rng, col : col + v.shape[1]] = v.astype(out.dtype)

        fold_piece(put, lambda g, col, k, w=w: w[g * third : (g + 1) * third, col : col + k], cols)


def fin2_kernel(idx, mine, other, gqkv, gout, gvec, ggain, ghid):
    c, core = idx[0], idx[1]
    parts, _, span = mine.shape
    hc = span // 3
    half = gqkv.shape[0] // 2
    width = gout.shape[1]
    piece = gout.shape[0] // parts
    cols = width // 2
    base = half + 16
    tot = mine[0, half:base, :].astype(F32)
    for k in range(1, parts):
        tot = tot + mine[k, half:base, :].astype(F32)
    for n in range(8):
        v = tot[n // 3 : n // 3 + 1, (n % 3) * hc : (n % 3 + 1) * hc]
        if n < 6:
            gvec[n : n + 1, :] = v
        else:
            ggain[n - 6 : n - 5, :] = v
    for j in range(parts):
        k = j ^ c
        ghid[:, j * hc : (j + 1) * hc] = mine[k, half:base, :].astype(F32)[2:3, 2 * hc :]
        for src, who in ((mine, core), (other, 1 - core)):
            v = src[k, :half, :].astype(F32)
            for s in range(3):
                gqkv[at(who * half, half, 32), s * width + j * hc : s * width + (j + 1) * hc] = v[
                    :, s * hc : (s + 1) * hc
                ]
            w = src[k, base:, :].astype(F32)
            third = piece // 3
            last = jnp.concatenate([w[:third, cols:], w[third:, cols:]], axis=1)
            for g, v in enumerate((w[:third, :cols], w[third:, :cols], last)):
                row = j * piece + g * third
                gout[row : row + third, at(who * cols, cols, 128)] = v


def call(kernel, out, *args, idx=None, scratch=(), hbm=(), after=(), limit=VMEM_BYTES):
    shapes = [jax.ShapeDtypeStruct(s, d) for s, d in out]
    specs = [
        pl.BlockSpec(memory_space=pltpu.HBM if n in hbm else pltpu.VMEM) for n in range(len(args))
    ]
    args = args + tuple(after)
    specs = specs + [pl.BlockSpec(memory_space=pl.ANY) for _ in after]
    skip = len(args) + (idx is not None)
    drop = len(after)

    def run(*refs):
        kernel(*refs[: skip - drop], *refs[skip:])

    if idx is not None:
        specs = [pl.BlockSpec(memory_space=pltpu.SMEM)] + specs
        args = (idx,) + args
    return pl.pallas_call(
        run if drop else kernel,
        out_shape=shapes,
        in_specs=specs,
        out_specs=[pl.BlockSpec(memory_space=pltpu.VMEM) for _ in shapes],
        scratch_shapes=[pltpu.VMEM(*s) if isinstance(s, tuple) else s for s in scratch],
        compiler_params=pltpu.CompilerParams(vmem_limit_bytes=limit),
        name=kernel.__name__,
        cost_estimate=pl.CostEstimate(flops=COST, bytes_accessed=100000, transcendentals=0),
    )(*args)


def gate(x, after):
    n = len(after)
    return pl.pallas_call(
        lambda *refs: None,
        out_shape=jax.ShapeDtypeStruct(x.shape, x.dtype),
        in_specs=[pl.BlockSpec(memory_space=pl.ANY)] * (n + 1),
        out_specs=pl.BlockSpec(memory_space=pl.ANY),
        input_output_aliases={0: 0},
        compiler_params=pltpu.CompilerParams(vmem_limit_bytes=VMEM_BYTES),
        name="gate_kernel",
    )(x, *after)


def make_body(reps, shards):
    def xor_perm(n, k):
        return [(i, i ^ k) for i in range(n)]

    def swap_core(v):
        return lax.ppermute(v, "rep", xor_perm(reps, 1))

    def swap_part(v, k):
        return lax.ppermute(v, "rep", xor_perm(reps, CORES * k))

    def swap_shard(v, k):
        return lax.ppermute(v, "shard", xor_perm(shards, k))

    def spread_part(v):
        return [v] + [swap_part(v, k) for k in range(1, PARTS)]

    def spread_shard(v):
        return [v] + [swap_shard(v, k) for k in range(1, shards)]

    def relay_shard(v):
        near, far = swap_shard(v, 1), swap_shard(v, 2)
        return [v, near, far, swap_shard(far, 1)]

    def trade_part(slots):
        return [slots[0]] + [swap_part(slots[k], k) for k in range(1, PARTS)]

    def trade_shard(slots):
        return [slots[0]] + [swap_shard(slots[k], k) for k in range(1, shards)]

    def total(slots):
        acc = slots[0]
        for s in slots[1:]:
            acc = acc + s.astype(F32)
        return acc

    def sum_outer(v):
        step = CORES * PARTS
        while step < reps:
            v = v + lax.ppermute(v, "rep", xor_perm(reps, step))
            step *= 2
        return v

    def body(
        tokens, w_qkv, w_out, w_up, w_down, vec_bias, ln_gain, hidden_bias, seq_lengths, cotangent
    ):
        rows, width = tokens.shape
        hid_own = hidden_bias.shape[0]
        wsh = width // shards
        half = wsh // CORES
        hc = width // PARTS
        fc = hid_own // PARTS
        span = 3 * hc
        piece = wsh // PARTS
        ocol = width // CORES
        rep = lax.axis_index("rep")
        z = lax.axis_index("shard")
        core = rep % CORES
        c = (rep // CORES) % PARTS
        idx = jnp.stack([c, core, z]).astype(jnp.int32)
        mats = [((rows, width), BF)]

        xp, pay1 = call(
            pack_kernel,
            [((rows + 16, width), BF), ((half + 16 + 2 * piece // 3, span), BF)],
            tokens,
            w_qkv,
            w_out,
            vec_bias,
            ln_gain,
            hidden_bias.reshape(1, hid_own),
            seq_lengths,
            idx=idx,
            hbm=range(7),
            limit=PACK_BYTES,
            scratch=[
                ((half, 3 * width), BF),
                ((piece, ocol), BF),
                (vec_bias.shape, BF),
                (ln_gain.shape, BF),
                ((1, hid_own), BF),
                (seq_lengths.shape, jnp.int32),
                pltpu.SemaphoreType.DMA((7,)),
            ],
        )
        got1 = relay_shard(pay1)
        xs = spread_part(xp)
        (pay2,) = call(
            pack2_kernel,
            [((half + fc // CORES, width), BF)],
            w_up,
            w_down,
            idx=idx,
            hbm=(0, 1),
            after=[xp],
            scratch=[((half, w_up.shape[1]), BF), pltpu.SemaphoreType.DMA((2,))],
        )
        pay2 = gate(pay2, [got1[3]] + xs[1:])
        got2 = relay_shard(pay2)
        mine1, pay_o = call(
            split_kernel,
            [((shards, half + 16, span), BF), ((shards, piece, ocol), BF)],
            *got1,
            after=[pay2],
        )
        other1 = swap_core(mine1)
        mine_o = jnp.stack(spread_part(pay_o))
        other_o = swap_core(mine_o)

        wq, small, bias = call(
            wq_kernel,
            [((width, span), BF), ((16, width), F32), ((8, span), F32)],
            mine1,
            other1,
            idx=idx,
            after=[pay2],
        )
        att = [
            call(
                attn_kernel,
                [((rows, span), BF), ((HEADS // PARTS, rows, rows), F32), ((rows, hc), BF)],
                x,
                wq,
                bias,
                after=[] if k else [mine_o],
            )
            for k, x in enumerate(xs)
        ]
        mix = trade_part([a[2] for a in att])
        (wo,) = call(wo_kernel, [((width, width), BF)], mine_o, other_o, idx=idx)
        y1, y1low, unit1, inv1 = call(
            out_kernel,
            [((rows, width), F32), ((rows, width), BF), ((rows, width), F32), ((rows, 128), F32)],
            tokens,
            *mix,
            wo,
            small,
            idx=idx,
            after=[got2[2]],
        )
        ys = spread_part(y1low)
        (mine2,) = call(
            join_kernel, [((shards,) + pay2.shape, BF)], *got2, after=ys[1:]
        )
        wu, wd = call(
            w2_kernel,
            [((width, shards * fc), BF), ((shards * fc, width), BF)],
            mine2,
            swap_core(mine2),
            idx=idx,
        )
        part_type = [F32] + [BF] * (PARTS - 1)
        ffn = [
            call(
                ffn_kernel,
                [((rows, shards * fc), BF), ((rows, shards * fc), F32), ((rows, width), t)],
                y,
                wu,
                wd,
                small,
            )
            for y, t in zip(ys, part_type)
        ]
        activations, dz, gh2, sm2 = call(
            ln2_kernel,
            mats * 2 + [((rows, width), F32), ((8, width), F32)],
            y1,
            *trade_part([f[2] for f in ffn]),
            small,
            cotangent,
            xp,
        )
        dzs = spread_part(dz)
        ffb = [
            call(
                ffb_kernel, [((rows, shards * fc), BF), ((rows, width), t)], d, wu, wd, f[1]
            )
            for d, f, t in zip(dzs, ffn, part_type)
        ]
        dyp = trade_part([f[1] for f in ffb])
        rows1 = half + fc // CORES
        give1, keep1, sm3 = call(
            ffw_kernel,
            [((shards, rows1, width), BF)] * 2 + [((8, shards * fc), F32)],
            *[f[0] for f in ffn],
            *dzs,
            *ys,
            *[f[0] for f in ffb],
            idx=idx,
            after=[dyp[3]],
            scratch=[((PARTS * rows, width), BF)] * 2 + [((width, width), BF)],
        )
        gh1, da, *rest = call(
            ln1b_kernel,
            [((rows, width), F32)] + mats + [((rows, hc), BF)] * PARTS + [((8, width), F32)],
            gh2,
            *dyp,
            unit1,
            inv1,
            small,
            wo,
            idx=idx,
            after=[give1],
        )
        dm, sm1 = trade_part(rest[:PARTS]), rest[PARTS]
        give_o, keep_o = call(
            outw_kernel,
            [((shards, wsh, ocol), BF)] * 2,
            *mix,
            da,
            idx=idx,
            after=[sm1],
        )
        out_send = call(
            oadd_kernel,
            [((shards, piece, ocol), F32)] + [((shards, piece, ocol), BF)] * 3,
            keep_o,
            swap_core(give_o),
            idx=idx,
        )
        osum = total(trade_part(out_send))

        def halve(keep, send, after):
            n, w = keep.shape[1:]
            own, far = call(
                add_far_kernel,
                [((n, w), F32), ((n, w), BF)],
                keep,
                swap_shard(send, 1),
                after=after,
            )
            return own, far

        def join(own, far, after):
            got = swap_shard(far, 2)
            if reps > CORES * PARTS:
                return sum_outer(own + got.astype(F32)).astype(BF)
            return call(sum_kernel, [(own.shape, BF)], own, got, after=after)[0]

        def spread_piece(v):
            done = jnp.stack(spread_part(v))
            return done, swap_core(done)

        def pair_shapes(n, w):
            return [((2, n, w), F32), ((2, n, w), BF)]

        keep_a, send_a = call(
            add_kernel,
            pair_shapes(rows1, width),
            keep1,
            swap_core(give1),
            idx=idx,
            after=[sm1],
        )
        dps = [
            call(
                attb_kernel,
                [((rows, span), BF)],
                d,
                a[0],
                a[1],
                after=[] if k else [send_a, give_o],
            )[0]
            for k, (d, a) in enumerate(zip(dm, att))
        ]
        rows2 = half + 16
        give2, keep2 = call(
            qw_kernel,
            [((shards, rows2, span), BF)] * 2,
            *xs,
            *dps,
            sm1,
            sm2,
            sm3,
            idx=idx,
            after=[out_send[0]],
            scratch=[
                ((PARTS * rows, width), BF),
                ((PARTS * rows, span), BF),
                ((width, span), BF),
            ],
        )
        keep_b, send_b = call(
            add2_kernel,
            pair_shapes(rows2 + 2 * piece // 3, span),
            keep2,
            swap_core(give2),
            osum,
            idx=idx,
        )
        dxp = call(
            dx_kernel, [((rows, width), t) for t in part_type], *dps, wq, after=[send_b]
        )
        dxp_got = trade_part(dxp)
        own_a, far_a = halve(keep_a, send_a, [send_b])
        own_b, far_b = halve(keep_b, send_b, [far_a])
        piece1 = join(own_a, far_a, dxp_got[1:] + [far_b])
        piece2 = join(own_b, far_b, [piece1])
        done1 = spread_piece(piece1)
        done2 = spread_piece(piece2)
        g_tok = gh1 + total(dxp_got)
        gw_up, gw_down = call(
            fin1_kernel, [(w_up.shape, F32), (w_down.shape, F32)], *done1, idx=idx, after=[piece2]
        )
        gw_qkv, gw_out, g_vec, g_gain, g_hidden = call(
            fin2_kernel,
            [
                (w_qkv.shape, F32),
                (w_out.shape, F32),
                ((6, wsh), F32),
                ((2, wsh), F32),
                ((1, hid_own), F32),
            ],
            *done2,
            idx=idx,
            after=[gw_up, g_tok],
        )
        return (
            activations,
            g_tok,
            gw_qkv,
            gw_out,
            gw_up,
            gw_down,
            g_vec,
            g_gain,
            g_hidden.reshape(hid_own),
        )

    return body


def solution(mesh):
    body = make_body(mesh.shape["rep"], mesh.shape["shard"])
    both = P(("rep", "shard"), None)
    first = P("shard", None)
    last = P(None, "shard")
    return jax.shard_map(
        body,
        mesh=mesh,
        in_specs=(both, first, first, first, first, last, last, P("shard"), both, both),
        out_specs=(both, both, first, first, first, first, last, last, P("shard")),
        check_vma=False,
    )
```

```python
import functools
import math

import jax
import jax.numpy as jnp
from jax import lax
from jax.experimental import pallas as pl
from jax.experimental.pallas import tpu as pltpu
from jax.sharding import PartitionSpec as P

HEADS = 12
HEAD_DIM = 64
PARTS = 4
CORES = 2
layer_eps = 1e-12
masked_score = -1000000000.0
BF = jnp.bfloat16
F32 = jnp.float32
VMEM_BYTES = 48 * 1024 * 1024
PACK_BYTES = 62 * 1024 * 1024
COST = 11 * 10**9


def mm(a, b):
    return jnp.dot(a, b, preferred_element_type=F32)


def mm_ta(a, b):
    return lax.dot_general(a, b, (((0,), (0,)), ((), ())), preferred_element_type=F32)


def mm_tb(a, b):
    return lax.dot_general(a, b, (((1,), (1,)), ((), ())), preferred_element_type=F32)


def at(start, size, unit):
    return pl.ds(pl.multiple_of(start, unit), size)


def norm_stats(h):
    centre = h - jnp.mean(h, axis=-1, keepdims=True)
    inv = lax.rsqrt(jnp.mean(centre * centre, axis=-1, keepdims=True) + layer_eps)
    return centre * inv, inv


def norm_back(g, unit, inv, gain):
    gg = g * gain
    m1 = jnp.mean(gg, axis=-1, keepdims=True)
    m2 = jnp.mean(gg * unit, axis=-1, keepdims=True)
    return inv * (gg - m1 - unit * m2)


def gelu_parts(u):
    phi = 0.5 * (1.0 + lax.erf(u * (1.0 / math.sqrt(2.0))))
    dens = jnp.exp(-0.5 * u * u) * (1.0 / math.sqrt(2.0 * math.pi))
    return phi, phi + u * dens


def col_sum(v):
    return jnp.sum(v, axis=0, keepdims=True)


def fold_piece(put, get, cols):
    put(0, 0, get(0, 0, cols))
    put(1, 0, get(1, 0, cols))
    put(0, cols, get(2, 0, cols // 2))
    put(1, cols, get(2, cols // 2, cols // 2))


def pack_kernel(idx, tok, wqkv, wout, vec_in, gain_in, hid_in, lens_in, xp, pay, bq, bo, vec, gain, hid, lens, sem):
    rows, width = tok.shape
    half = bq.shape[0]
    piece, ocol = bo.shape
    hc = width // PARTS
    fc = hid.shape[1] // PARTS
    load_q = pltpu.make_async_copy(wqkv.at[at(idx[1] * half, half, 32)], bq, sem.at[0])
    load_o = pltpu.make_async_copy(
        wout.at[at(idx[0] * piece, piece, 16), at(idx[1] * ocol, ocol, 128)], bo, sem.at[1]
    )
    load_x = pltpu.make_async_copy(tok, xp.at[:rows], sem.at[2])
    small = [
        pltpu.make_async_copy(a, b, sem.at[3 + n])
        for n, (a, b) in enumerate(
            ((vec_in, vec), (gain_in, gain), (hid_in, hid), (lens_in, lens))
        )
    ]
    load_q.start()
    load_x.start()
    load_o.start()
    for load in small:
        load.start()
    base = half + 16
    pay[half:base] = jnp.zeros((16, 3 * hc), BF)
    xp[rows:] = jnp.zeros((16, width), BF)
    for load in small:
        load.wait()
    xp[rows : rows + 1, : lens.shape[1]] = lens[...].astype(BF)
    for n in range(8):
        src = vec[n : n + 1, :] if n < 6 else gain[n - 6 : n - 5, :]
        pay[half + n // 3 : half + n // 3 + 1, (n % 3) * hc : (n % 3 + 1) * hc] = src
    load_o.wait()
    third = piece // 3

    def put(row, col, v):
        pay[base + row * third : base + (row + 1) * third, col : col + v.shape[1]] = v

    fold_piece(put, lambda g, col, n: bo[g * third : (g + 1) * third, col : col + n], ocol)
    load_q.wait()
    for j in range(PARTS):

        @pl.when(idx[0] == j)
        def _(j=j):
            pay[half + 2 : half + 3, 2 * hc :] = hid[:, j * fc : (j + 1) * fc]
            for s in range(3):
                pay[:half, s * hc : (s + 1) * hc] = bq[
                    :, s * width + j * hc : s * width + (j + 1) * hc
                ]

    load_x.wait()


def pack2_kernel(idx, wup, wdown, pay, bu, sem):
    half = bu.shape[0]
    fc = pay.shape[0] - half
    units = wdown.shape[0]
    shards = wup.shape[1] // units
    fpart = units // PARTS
    load_u = pltpu.make_async_copy(wup.at[at(idx[1] * half, half, 32)], bu, sem.at[0])
    load_d = pltpu.make_async_copy(
        wdown.at[at(idx[0] * fpart + idx[1] * fc, fc, 32)], pay.at[half:], sem.at[1]
    )
    load_u.start()
    load_d.start()
    load_u.wait()
    for j in range(PARTS):

        @pl.when(idx[0] == j)
        def _(j=j):
            for s in range(shards):
                base = (s * PARTS + j) * fpart
                pay[:half, s * fpart : (s + 1) * fpart] = bu[:, base : base + fpart]

    load_d.wait()


def split_kernel(g0, g1, g2, g3, first, second):
    base = first.shape[1]
    cols = second.shape[2]
    third = second.shape[1] // 3
    for k, g in enumerate((g0, g1, g2, g3)):
        first[k] = g[:base, :]
        top, low = g[base : base + third, :], g[base + third :, :]
        second[k, :third] = top[:, :cols]
        second[k, third : 2 * third] = low[:, :cols]
        second[k, 2 * third :, : cols // 2] = top[:, cols:]
        second[k, 2 * third :, cols // 2 :] = low[:, cols:]


def sum_kernel(*refs):
    out = refs[-1]
    v = refs[0][...].astype(F32)
    for r in refs[1:-1]:
        v = v + r[...].astype(F32)
    out[...] = v.astype(out.dtype)


def wq_kernel(idx, mine, other, wq, small, bias):
    c, core, z = idx[0], idx[1], idx[2]
    shards, _, span = mine.shape
    hc = span // 3
    half = wq.shape[0] // shards // CORES
    for m in range(shards):
        base = (z ^ m) * (CORES * half)
        wq[at(base + core * half, half, 32), :] = mine[m, :half, :]
        wq[at(base + (1 - core) * half, half, 32), :] = other[m, :half, :]
    small[...] = jnp.zeros_like(small)
    for j in range(shards):
        e = mine[j ^ z, half:, :].astype(F32)
        for n in range(9):
            small[n : n + 1, j * hc : (j + 1) * hc] = e[
                n // 3 : n // 3 + 1, (n % 3) * hc : (n % 3 + 1) * hc
            ]
    e = mine[c ^ z, half:, :].astype(F32)[:1]
    row = jnp.concatenate([e[:, :hc], jnp.zeros((1, hc), F32), e[:, hc : 2 * hc]], axis=1)
    bias[...] = jnp.broadcast_to(row, bias.shape)


def attn_kernel(x, wq, bias, pj, probs, out):
    rows, span = pj.shape
    hc = span // 3
    heads = hc // HEAD_DIM
    scale = 1.0 / math.sqrt(HEAD_DIM)
    pj[...] = (mm(x[:rows, :], wq[...]) + bias[:1, :]).astype(BF)
    pos_r = lax.broadcasted_iota(jnp.int32, (rows, 1), 0).astype(F32)
    pos_c = lax.broadcasted_iota(jnp.int32, (1, rows), 1).astype(F32)
    lens = x[rows : rows + 16, :128].astype(F32)[:1]
    end = jnp.zeros((1, 1), F32)
    seg_r = jnp.zeros((rows, 1), F32)
    seg_c = jnp.zeros((1, rows), F32)
    for n in range(3):
        end = end + lens[:, n : n + 1]
        seg_r = seg_r + (pos_r >= end).astype(F32)
        seg_c = seg_c + (pos_c >= end).astype(F32)
    same = seg_r == seg_c
    pb = pj[...]
    mixes = []
    for h in range(heads):
        q = pb[:, h * HEAD_DIM : (h + 1) * HEAD_DIM]
        k = pb[:, hc + h * HEAD_DIM : hc + (h + 1) * HEAD_DIM]
        v = pb[:, 2 * hc + h * HEAD_DIM : 2 * hc + (h + 1) * HEAD_DIM]
        s = jnp.where(same, mm_tb(q, k) * scale, masked_score)
        e = jnp.exp(s - jnp.max(s, axis=-1, keepdims=True))
        p = e / jnp.sum(e, axis=-1, keepdims=True)
        probs[h] = p
        mixes.append(mm(p.astype(BF), v))
    out[...] = jnp.concatenate(mixes, axis=1).astype(BF)


def wo_kernel(idx, mine, other, wo):
    c, core, z = idx[0], idx[1], idx[2]
    parts, shards, piece, cols = mine.shape
    for k in range(parts):
        for m in range(shards):
            base = at((z ^ m) * (parts * piece) + (c ^ k) * piece, piece, 16)
            wo[base, at(core * cols, cols, 128)] = mine[k, m]
            wo[base, at((1 - core) * cols, cols, 128)] = other[k, m]


def out_kernel(idx, tok, m0, m1, m2, m3, wo, small, y1, y1low, unit, inv):
    c = idx[0]
    hc = m0.shape[1]
    acc = small[2:3, :]
    for k, m in enumerate((m0, m1, m2, m3)):
        acc = acc + mm(m[...], wo[at((c ^ k) * hc, hc, 64), :])
    u, r = norm_stats(tok[...].astype(F32) + acc)
    unit[...] = u
    inv[...] = jnp.broadcast_to(r, inv.shape)
    y = u * small[6:7, :] + small[3:4, :]
    y1[...] = y
    y1low[...] = y.astype(BF)


def join_kernel(near, far, out):
    out[:2] = near[...]
    out[2:] = far[...]


def stack_kernel(g0, g1, g2, g3, out):
    for k, g in enumerate((g0, g1, g2, g3)):
        out[k] = g[...]


def w2_kernel(idx, mine, other, wu, wd):
    core, z = idx[1], idx[2]
    half = mine.shape[1] // 2
    for m in range(mine.shape[0]):
        base = (z ^ m) * (2 * half)
        lo = at(base + core * half, half, 32)
        hi = at(base + (1 - core) * half, half, 32)
        wu[lo, :] = mine[m, :half, :]
        wu[hi, :] = other[m, :half, :]
        wd[lo, :] = mine[m, half:, :]
        wd[hi, :] = other[m, half:, :]


def ffn_kernel(y, wu, wd, small, act, slope, out):
    u = mm(y[...], wu[...]) + small[8:9, :]
    phi, slp = gelu_parts(u)
    a = (u * phi).astype(BF)
    act[...] = a
    slope[...] = slp
    out[...] = mm(a, wd[...]).astype(out.dtype)


def ln2_kernel(y1, z0, r1, r2, r3, small, cot, x0, actv, dz, gh2, sm):
    rows = y1.shape[0]
    branch = z0[...] + r1[...].astype(F32) + r2[...].astype(F32) + r3[...].astype(F32)
    u, r = norm_stats(y1[...] + (branch + small[4:5, :]))
    lens = x0[rows : rows + 16, :128].astype(F32)[:1]
    total = lens[:, 0:1] + lens[:, 1:2] + lens[:, 2:3]
    keep = (lax.broadcasted_iota(jnp.int32, (rows, 1), 0).astype(F32) < total).astype(F32)
    actv[...] = ((u * small[7:8, :] + small[5:6, :]) * keep).astype(BF)
    g = cot[...].astype(F32) * keep
    gh = norm_back(g, u, r, small[7:8, :])
    gh2[...] = gh
    low = gh.astype(BF)
    dz[...] = low
    sm[...] = jnp.zeros_like(sm)
    sm[0:1, :] = col_sum(low.astype(F32))
    sm[1:2, :] = col_sum(g)
    sm[2:3, :] = col_sum(g * u)


def ffb_kernel(d, wu, wd, slope, du, out):
    t = (mm_tb(d[...], wd[...]) * slope[...]).astype(BF)
    du[...] = t
    out[...] = mm_tb(t, wu[...]).astype(out.dtype)


def ffw_kernel(idx, *refs):
    core = idx[1]
    groups = [refs[n * PARTS : (n + 1) * PARTS] for n in range(4)]
    give, mine, hid, left, right, full = refs[4 * PARTS :]
    rows, width = groups[0][0].shape
    shards = give.shape[0]
    half = width // shards // CORES
    acts, dzs, ys, dus = groups
    h = None
    for base, lefts, rights in ((0, ys, dus), (half, acts, dzs)):
        for k in range(PARTS):
            left[k * rows : (k + 1) * rows, :] = lefts[k][...]
            right[k * rows : (k + 1) * rows, :] = rights[k][...]
        if base == 0:
            h = col_sum(right[...].astype(F32))
        full[...] = mm_ta(left[...], right[...]).astype(BF)
        for j in range(shards):
            mine[j, base : base + half, :] = full[at(j * 2 * half + core * half, half, 32), :]
            give[j, base : base + half, :] = full[
                at(j * 2 * half + (1 - core) * half, half, 32), :
            ]
    hid[...] = jnp.broadcast_to(h, hid.shape)


def add_kernel(idx, mine, got, own, near, far, send):
    z = idx[2]
    for k, out in enumerate((own, near, far, send)):
        out[...] = (mine[z ^ k].astype(F32) + got[z ^ k].astype(F32)).astype(out.dtype)


def fin1_kernel(idx, mine, other, gup, gdown, token):
    c, core = idx[0], idx[1]
    parts, _, width = mine.shape
    half = gup.shape[0] // 2
    fc = gdown.shape[0] // parts
    shards = gup.shape[1] // (parts * fc)
    for j in range(parts):
        k = j ^ c
        token[...] = jnp.zeros_like(token)
        for src, row in ((mine, core * half), (other, (1 - core) * half)):
            v = src[k, :half, :].astype(F32)
            for s in range(shards):
                base = (s * parts + j) * fc
                gup[at(row, half, 32), base : base + fc] = v[:, s * fc : (s + 1) * fc]
            gdown[at(j * fc + row, half, 32), :] = src[k, half : 2 * half, :].astype(F32)


def ln1b_kernel(idx, gh2, o0, r1, r2, r3, unit, inv, small, wo, gh1, da, m0, m1, m2, m3, sm):
    c = idx[0]
    hc = m0.shape[1]
    dy = gh2[...] + o0[...] + r1[...].astype(F32) + r2[...].astype(F32) + r3[...].astype(F32)
    u = unit[...]
    gh = norm_back(dy, u, inv[:, :1], small[6:7, :])
    gh1[...] = gh
    low = gh.astype(BF)
    da[...] = low
    for k, m in enumerate((m0, m1, m2, m3)):
        m[...] = mm_tb(low, wo[at((c ^ k) * hc, hc, 64), :]).astype(BF)
    sm[...] = jnp.zeros_like(sm)
    sm[0:1, :] = col_sum(low.astype(F32))
    sm[1:2, :] = col_sum(dy)
    sm[2:3, :] = col_sum(dy * u)


def outw_kernel(idx, m0, m1, m2, m3, da, give, mine):
    c, core = idx[0], idx[1]
    cols = give.shape[2]
    lo, hi = da[:, :cols], da[:, cols:]
    first = core == 0
    keep = jnp.where(first, lo.astype(F32), hi.astype(F32)).astype(BF)
    pass_on = jnp.where(first, hi.astype(F32), lo.astype(F32)).astype(BF)
    for k, m in enumerate((m0, m1, m2, m3)):
        mine[c ^ k] = mm_ta(m[...], keep).astype(BF)
        give[c ^ k] = mm_ta(m[...], pass_on).astype(BF)


def oadd_kernel(idx, mine, got, own, s1, s2, s3):
    c = idx[0]
    shards, piece = own.shape[0], own.shape[1]
    for k, out in enumerate((own, s1, s2, s3)):
        rng = at((c ^ k) * piece, piece, 16)
        for j in range(shards):
            v = mine[j, rng, :].astype(F32) + got[j, rng, :].astype(F32)
            out[j] = v.astype(out.dtype)


def attb_kernel(d, pj, probs, dp):
    rows, hc = d.shape
    heads = hc // HEAD_DIM
    scale = 1.0 / math.sqrt(HEAD_DIM)
    pb = pj[...]
    db = d[...]
    dqs, dks, dvs = [], [], []
    for h in range(heads):
        q = pb[:, h * HEAD_DIM : (h + 1) * HEAD_DIM]
        k = pb[:, hc + h * HEAD_DIM : hc + (h + 1) * HEAD_DIM]
        v = pb[:, 2 * hc + h * HEAD_DIM : 2 * hc + (h + 1) * HEAD_DIM]
        g = db[:, h * HEAD_DIM : (h + 1) * HEAD_DIM]
        p = probs[h]
        dvs.append(mm_ta(p.astype(BF), g))
        dpr = mm_tb(g, v)
        inner = jnp.sum(p * dpr, axis=-1, keepdims=True)
        ds = (p * (dpr - inner)).astype(BF)
        dqs.append(mm(ds, k) * scale)
        dks.append(mm_ta(ds, q) * scale)
    dp[...] = jnp.concatenate(dqs + dks + dvs, axis=1).astype(BF)


def dx_kernel(d0, d1, d2, d3, wq, o0, o1, o2, o3):
    for d, out in ((d0, o0), (d1, o1), (d2, o2), (d3, o3)):
        out[...] = mm_tb(d[...], wq[...]).astype(out.dtype)


def qw_kernel(idx, x0, x1, x2, x3, d0, d1, d2, d3, sm1, sm2, hid, give, mine, xg, dp, full):
    c, core = idx[0], idx[1]
    shards, _, span = give.shape
    rows = d0.shape[0]
    hc = span // 3
    half = xg.shape[1] // shards // CORES
    for k, (x, d) in enumerate(((x0, d0), (x1, d1), (x2, d2), (x3, d3))):
        xg[k * rows : (k + 1) * rows, :] = x[:rows, :]
        dp[k * rows : (k + 1) * rows, :] = d[...]
    full[...] = mm_ta(xg[...], dp[...]).astype(BF)
    cols = col_sum(dp[...].astype(F32))
    vecs = (sm1[0:1], sm1[1:2], sm2[0:1], sm2[1:2], sm1[2:3], sm2[2:3])
    for j in range(shards):
        mine[j, :half, :] = full[at(j * 2 * half + core * half, half, 32), :]
        give[j, :half, :] = full[at(j * 2 * half + (1 - core) * half, half, 32), :]
        part = [v[:, j * hc : (j + 1) * hc] for v in vecs]
        own = jnp.where(c == j, 1.0, 0.0)
        rows = jnp.concatenate(
            [
                jnp.concatenate([cols[:, :hc] * own, cols[:, 2 * hc :] * own, part[0]], axis=1),
                jnp.concatenate(part[1:4], axis=1),
                jnp.concatenate(part[4:6] + [hid[:1, j * hc : (j + 1) * hc]], axis=1),
                jnp.zeros((13, span), F32),
            ],
            axis=0,
        ).astype(BF)
        mine[j, half:, :] = rows
        give[j, half:, :] = rows


def add2_kernel(idx, mine, got, osum, own, near, far, send):
    z = idx[2]
    base, _ = mine.shape[1:]
    piece, cols = osum.shape[1:]
    third = piece // 3
    for n, out in enumerate((own, near, far, send)):
        j = z ^ n
        out[:base, :] = (mine[j].astype(F32) + got[j].astype(F32)).astype(out.dtype)
        w = osum[j]

        def put(row, col, v, out=out):
            rng = slice(base + row * third, base + (row + 1) * third)
            out[rng, col : col + v.shape[1]] = v.astype(out.dtype)

        fold_piece(put, lambda g, col, k, w=w: w[g * third : (g + 1) * third, col : col + k], cols)


def fin2_kernel(idx, mine, other, gqkv, gout, gvec, ggain, ghid):
    c, core = idx[0], idx[1]
    parts, _, span = mine.shape
    hc = span // 3
    half = gqkv.shape[0] // 2
    width = gout.shape[1]
    piece = gout.shape[0] // parts
    cols = width // 2
    base = half + 16
    tot = mine[0, half:base, :].astype(F32)
    for k in range(1, parts):
        tot = tot + mine[k, half:base, :].astype(F32)
    for n in range(8):
        v = tot[n // 3 : n // 3 + 1, (n % 3) * hc : (n % 3 + 1) * hc]
        if n < 6:
            gvec[n : n + 1, :] = v
        else:
            ggain[n - 6 : n - 5, :] = v
    for j in range(parts):
        k = j ^ c
        ghid[:, j * hc : (j + 1) * hc] = mine[k, half:base, :].astype(F32)[2:3, 2 * hc :]
        for src, who in ((mine, core), (other, 1 - core)):
            v = src[k, :half, :].astype(F32)
            for s in range(3):
                gqkv[at(who * half, half, 32), s * width + j * hc : s * width + (j + 1) * hc] = v[
                    :, s * hc : (s + 1) * hc
                ]
            w = src[k, base:, :].astype(F32)
            third = piece // 3
            last = jnp.concatenate([w[:third, cols:], w[third:, cols:]], axis=1)
            for g, v in enumerate((w[:third, :cols], w[third:, :cols], last)):
                row = j * piece + g * third
                gout[row : row + third, at(who * cols, cols, 128)] = v


def call(kernel, out, *args, idx=None, scratch=(), hbm=(), after=(), limit=VMEM_BYTES):
    shapes = [jax.ShapeDtypeStruct(s, d) for s, d in out]
    specs = [
        pl.BlockSpec(memory_space=pltpu.HBM if n in hbm else pltpu.VMEM) for n in range(len(args))
    ]
    args = args + tuple(after)
    specs = specs + [pl.BlockSpec(memory_space=pl.ANY) for _ in after]
    skip = len(args) + (idx is not None)
    drop = len(after)

    def run(*refs):
        kernel(*refs[: skip - drop], *refs[skip:])

    if idx is not None:
        specs = [pl.BlockSpec(memory_space=pltpu.SMEM)] + specs
        args = (idx,) + args
    return pl.pallas_call(
        run if drop else kernel,
        out_shape=shapes,
        in_specs=specs,
        out_specs=[pl.BlockSpec(memory_space=pltpu.VMEM) for _ in shapes],
        scratch_shapes=[pltpu.VMEM(*s) if isinstance(s, tuple) else s for s in scratch],
        compiler_params=pltpu.CompilerParams(vmem_limit_bytes=limit),
        name=kernel.__name__,
        cost_estimate=pl.CostEstimate(flops=COST, bytes_accessed=100000, transcendentals=0),
    )(*args)


def gate(x, after):
    n = len(after)
    return pl.pallas_call(
        lambda *refs: None,
        out_shape=jax.ShapeDtypeStruct(x.shape, x.dtype),
        in_specs=[pl.BlockSpec(memory_space=pl.ANY)] * (n + 1),
        out_specs=pl.BlockSpec(memory_space=pl.ANY),
        input_output_aliases={0: 0},
        compiler_params=pltpu.CompilerParams(vmem_limit_bytes=VMEM_BYTES),
        name="gate_kernel",
    )(x, *after)


def make_body(reps, shards):
    def xor_perm(n, k):
        return [(i, i ^ k) for i in range(n)]

    def swap_core(v):
        return lax.ppermute(v, "rep", xor_perm(reps, 1))

    def swap_part(v, k):
        return lax.ppermute(v, "rep", xor_perm(reps, CORES * k))

    def swap_shard(v, k):
        return lax.ppermute(v, "shard", xor_perm(shards, k))

    def spread_part(v):
        return [v] + [swap_part(v, k) for k in range(1, PARTS)]

    def spread_shard(v):
        return [v] + [swap_shard(v, k) for k in range(1, shards)]

    def relay_shard(v, after=None):
        near, far = swap_shard(v, 1), swap_shard(v, 2)
        if after is not None:
            far = gate(far, after())
        return [v, near, far, swap_shard(far, 1)]

    def trade_part(slots):
        return [slots[0]] + [swap_part(slots[k], k) for k in range(1, PARTS)]

    def trade_shard(slots):
        return [slots[0]] + [swap_shard(slots[k], k) for k in range(1, shards)]

    def total(slots):
        acc = slots[0]
        for s in slots[1:]:
            acc = acc + s.astype(F32)
        return acc

    def sum_outer(v):
        step = CORES * PARTS
        while step < reps:
            v = v + lax.ppermute(v, "rep", xor_perm(reps, step))
            step *= 2
        return v

    def body(
        tokens, w_qkv, w_out, w_up, w_down, vec_bias, ln_gain, hidden_bias, seq_lengths, cotangent
    ):
        rows, width = tokens.shape
        hid_own = hidden_bias.shape[0]
        wsh = width // shards
        half = wsh // CORES
        hc = width // PARTS
        fc = hid_own // PARTS
        span = 3 * hc
        piece = wsh // PARTS
        ocol = width // CORES
        rep = lax.axis_index("rep")
        z = lax.axis_index("shard")
        core = rep % CORES
        c = (rep // CORES) % PARTS
        idx = jnp.stack([c, core, z]).astype(jnp.int32)
        mats = [((rows, width), BF)]

        xp, pay1 = call(
            pack_kernel,
            [((rows + 16, width), BF), ((half + 16 + 2 * piece // 3, span), BF)],
            tokens,
            w_qkv,
            w_out,
            vec_bias,
            ln_gain,
            hidden_bias.reshape(1, hid_own),
            seq_lengths,
            idx=idx,
            hbm=range(7),
            limit=PACK_BYTES,
            scratch=[
                ((half, 3 * width), BF),
                ((piece, ocol), BF),
                (vec_bias.shape, BF),
                (ln_gain.shape, BF),
                ((1, hid_own), BF),
                (seq_lengths.shape, jnp.int32),
                pltpu.SemaphoreType.DMA((7,)),
            ],
        )
        xs = spread_part(xp)
        got1 = relay_shard(pay1, lambda: [xs[3]])
        (pay2,) = call(
            pack2_kernel,
            [((half + fc // CORES, width), BF)],
            w_up,
            w_down,
            idx=idx,
            hbm=(0, 1),
            after=[xp],
            scratch=[((half, w_up.shape[1]), BF), pltpu.SemaphoreType.DMA((2,))],
        )
        pay2 = gate(pay2, [got1[3]] + xs[1:])
        mine1, pay_o = call(
            split_kernel,
            [((shards, half + 16, span), BF), ((shards, piece, ocol), BF)],
            *got1,
        )
        other1 = swap_core(mine1)
        pair_o = jnp.stack([pay_o, swap_part(pay_o, 1)])
        far_o = swap_part(pair_o, 2)

        wq, small, bias = call(
            wq_kernel,
            [((width, span), BF), ((16, width), F32), ((8, span), F32)],
            mine1,
            other1,
            idx=idx,
            after=[pay2],
        )
        att = [
            call(
                attn_kernel,
                [((rows, span), BF), ((HEADS // PARTS, rows, rows), F32), ((rows, hc), BF)],
                x,
                wq,
                bias,
            )
            for k, x in enumerate(xs)
        ]
        mix = trade_part([a[2] for a in att])
        got2 = relay_shard(pay2, lambda: mix[1:])
        (mine_o,) = call(
            join_kernel, [((PARTS,) + pay_o.shape, BF)], pair_o, far_o, after=[att[3][2]]
        )
        other_o = swap_core(mine_o)
        (wo,) = call(wo_kernel, [((width, width), BF)], mine_o, other_o, idx=idx)
        y1, y1low, unit1, inv1 = call(
            out_kernel,
            [((rows, width), F32), ((rows, width), BF), ((rows, width), F32), ((rows, 128), F32)],
            tokens,
            *mix,
            wo,
            small,
            idx=idx,
        )
        ys = spread_part(y1low)
        (mine2,) = call(
            stack_kernel, [((shards,) + pay2.shape, BF)], *got2, after=ys[1:]
        )
        wu, wd = call(
            w2_kernel,
            [((width, shards * fc), BF), ((shards * fc, width), BF)],
            mine2,
            swap_core(mine2),
            idx=idx,
        )
        part_type = [F32] + [BF] * (PARTS - 1)
        ffn = [
            call(
                ffn_kernel,
                [((rows, shards * fc), BF), ((rows, shards * fc), F32), ((rows, width), t)],
                y,
                wu,
                wd,
                small,
            )
            for y, t in zip(ys, part_type)
        ]
        activations, dz, gh2, sm2 = call(
            ln2_kernel,
            mats * 2 + [((rows, width), F32), ((8, width), F32)],
            y1,
            *trade_part([f[2] for f in ffn]),
            small,
            cotangent,
            xp,
        )
        dzs = spread_part(dz)
        ffb = [
            call(
                ffb_kernel, [((rows, shards * fc), BF), ((rows, width), t)], d, wu, wd, f[1]
            )
            for d, f, t in list(zip(dzs, ffn, part_type))[1:]
        ]
        ffb = [
            call(
                ffb_kernel,
                [((rows, shards * fc), BF), ((rows, width), F32)],
                dz,
                wu,
                wd,
                ffn[0][1],
                after=[f[0] for f in ffb],
            )
        ] + ffb
        dyp = trade_part([f[1] for f in ffb])
        rows1 = half + fc // CORES
        give1, keep1, sm3 = call(
            ffw_kernel,
            [((shards, rows1, width), BF)] * 2 + [((8, shards * fc), F32)],
            *[f[0] for f in ffn],
            *dzs,
            *ys,
            *[f[0] for f in ffb],
            idx=idx,
            after=[dyp[3]],
            scratch=[((PARTS * rows, width), BF)] * 2 + [((width, width), BF)],
        )
        def relay_sum(far, send, after):
            got = swap_shard(send, 1)
            (low,) = call(sum_kernel, [(far.shape, BF)], far, got, after=after)
            return low, swap_shard(low, 2)

        def join(own, near, far, after):
            if reps > CORES * PARTS:
                return sum_outer(own + near.astype(F32) + far.astype(F32)).astype(BF)
            return call(sum_kernel, [(own.shape, BF)], own, near, far, after=after)[0]

        def spread_piece(v, after):
            (done,) = call(
                stack_kernel, [((PARTS,) + v.shape, BF)], *spread_part(v), after=after
            )
            return done, swap_core(done)

        def pair_shapes(n, w):
            return [((n, w), F32), ((n, w), BF), ((n, w), F32), ((n, w), BF)]

        own_a, near_a, far_a, send_a = call(
            add_kernel,
            pair_shapes(rows1, width),
            keep1,
            swap_core(give1),
            idx=idx,
            after=[dyp[3]],
        )
        gh1, da, *rest = call(
            ln1b_kernel,
            [((rows, width), F32)] + mats + [((rows, hc), BF)] * PARTS + [((8, width), F32)],
            gh2,
            *dyp,
            unit1,
            inv1,
            small,
            wo,
            idx=idx,
            after=[send_a],
        )
        dm, sm1 = trade_part(rest[:PARTS]), rest[PARTS]
        give_o, keep_o = call(
            outw_kernel,
            [((shards, wsh, ocol), BF)] * 2,
            *mix,
            da,
            idx=idx,
            after=[sm1],
        )
        out_send = call(
            oadd_kernel,
            [((shards, piece, ocol), F32)] + [((shards, piece, ocol), BF)] * 3,
            keep_o,
            swap_core(give_o),
            idx=idx,
        )
        out_got = trade_part(out_send)
        osum = total(out_got)

        dps = [
            call(
                attb_kernel,
                [((rows, span), BF)],
                d,
                a[0],
                a[1],
                after=[out_send[0]] if k < 2 else [],
            )[0]
            for k, (d, a) in enumerate(zip(dm, att))
        ]
        low_a, got_a = relay_sum(far_a, send_a, [dps[3]])
        near_a = swap_shard(gate(near_a, [low_a]), 1)
        rows2 = half + 16
        give2, keep2 = call(
            qw_kernel,
            [((shards, rows2, span), BF)] * 2,
            *xs,
            *dps,
            sm1,
            sm2,
            sm3,
            idx=idx,
            after=[out_got[1], low_a],
            scratch=[
                ((PARTS * rows, width), BF),
                ((PARTS * rows, span), BF),
                ((width, span), BF),
            ],
        )
        dxp = call(
            dx_kernel, [((rows, width), t) for t in part_type], *dps, wq, after=[give2] + out_got[2:]
        )
        dxp_got = trade_part(dxp)
        own_b, near_b, far_b, send_b = call(
            add2_kernel,
            pair_shapes(rows2 + 2 * piece // 3, span),
            keep2,
            swap_core(give2),
            osum,
            idx=idx,
            after=[got_a, dxp[0]],
        )
        low_b, got_b = relay_sum(far_b, send_b, dxp_got[1:])
        near_b = swap_shard(gate(near_b, [low_b]), 1)
        piece1 = join(own_a, near_a, got_a, [low_b])
        done1 = spread_piece(piece1, [got_b, near_b])
        piece2 = join(own_b, near_b, got_b, [])
        done2 = spread_piece(piece2, [])
        g_tok = gh1 + total(dxp_got)
        gw_up, gw_down, token = call(
            fin1_kernel, [(w_up.shape, F32), (w_down.shape, F32), ((8, 128), F32)], *done1, idx=idx, after=[piece2]
        )
        gw_qkv, gw_out, g_vec, g_gain, g_hidden = call(
            fin2_kernel,
            [
                (w_qkv.shape, F32),
                (w_out.shape, F32),
                ((6, wsh), F32),
                ((2, wsh), F32),
                ((1, hid_own), F32),
            ],
            *done2,
            idx=idx,
            after=[token, g_tok],
        )
        return (
            activations,
            g_tok,
            gw_qkv,
            gw_out,
            gw_up,
            gw_down,
            g_vec,
            g_gain,
            g_hidden.reshape(hid_own),
        )

    return body


def solution(mesh):
    body = make_body(mesh.shape["rep"], mesh.shape["shard"])
    both = P(("rep", "shard"), None)
    first = P("shard", None)
    last = P(None, "shard")
    return jax.shard_map(
        body,
        mesh=mesh,
        in_specs=(both, first, first, first, first, last, last, P("shard"), both, both),
        out_specs=(both, both, first, first, first, first, last, last, P("shard")),
        check_vma=False,
    )
```

```python
import functools
import math

import jax
import jax.numpy as jnp
from jax import lax
from jax.experimental import pallas as pl
from jax.experimental.pallas import tpu as pltpu
from jax.sharding import PartitionSpec as P

HEADS = 12
HEAD_DIM = 64
PARTS = 4
CORES = 2
layer_eps = 1e-12
masked_score = -1000000000.0
BF = jnp.bfloat16
F32 = jnp.float32
VMEM_BYTES = 48 * 1024 * 1024
PACK_BYTES = 62 * 1024 * 1024
COST = 11 * 10**9


def mm(a, b):
    return jnp.dot(a, b, preferred_element_type=F32)


def mm_ta(a, b):
    return lax.dot_general(a, b, (((0,), (0,)), ((), ())), preferred_element_type=F32)


def mm_tb(a, b):
    return lax.dot_general(a, b, (((1,), (1,)), ((), ())), preferred_element_type=F32)


def at(start, size, unit):
    return pl.ds(pl.multiple_of(start, unit), size)


def norm_stats(h):
    centre = h - jnp.mean(h, axis=-1, keepdims=True)
    inv = lax.rsqrt(jnp.mean(centre * centre, axis=-1, keepdims=True) + layer_eps)
    return centre * inv, inv


def norm_back(g, unit, inv, gain):
    gg = g * gain
    m1 = jnp.mean(gg, axis=-1, keepdims=True)
    m2 = jnp.mean(gg * unit, axis=-1, keepdims=True)
    return inv * (gg - m1 - unit * m2)


def gelu_parts(u):
    phi = 0.5 * (1.0 + lax.erf(u * (1.0 / math.sqrt(2.0))))
    dens = jnp.exp(-0.5 * u * u) * (1.0 / math.sqrt(2.0 * math.pi))
    return phi, phi + u * dens


def col_sum(v):
    return jnp.sum(v, axis=0, keepdims=True)


def fold_piece(put, get, cols):
    put(0, 0, get(0, 0, cols))
    put(1, 0, get(1, 0, cols))
    put(0, cols, get(2, 0, cols // 2))
    put(1, cols, get(2, cols // 2, cols // 2))


def pack_kernel(idx, tok, wqkv, wout, vec_in, gain_in, hid_in, lens_in, xp, pay, bq, bo, vec, gain, hid, lens, sem):
    rows, width = tok.shape
    half = bq.shape[0]
    piece, ocol = bo.shape
    hc = width // PARTS
    fc = hid.shape[0] // PARTS
    load_q = pltpu.make_async_copy(wqkv.at[at(idx[1] * half, half, 32)], bq, sem.at[0])
    load_o = pltpu.make_async_copy(
        wout.at[at(idx[0] * piece, piece, 16), at(idx[1] * ocol, ocol, 128)], bo, sem.at[1]
    )
    load_x = pltpu.make_async_copy(tok, xp.at[:rows], sem.at[2])
    small = [
        pltpu.make_async_copy(a, b, sem.at[3 + n])
        for n, (a, b) in enumerate(
            ((vec_in, vec), (gain_in, gain), (hid_in, hid), (lens_in, lens))
        )
    ]
    load_q.start()
    load_x.start()
    load_o.start()
    for load in small:
        load.start()
    base = half + 16
    pay[half:base] = jnp.zeros((16, 3 * hc), BF)
    xp[rows:] = jnp.zeros((16, width), BF)
    for load in small:
        load.wait()
    xp[rows : rows + 1, : lens.shape[1]] = lens[...].astype(BF)
    for n in range(8):
        src = vec[n : n + 1, :] if n < 6 else gain[n - 6 : n - 5, :]
        pay[half + n // 3 : half + n // 3 + 1, (n % 3) * hc : (n % 3 + 1) * hc] = src
    load_o.wait()
    third = piece // 3

    def put(row, col, v):
        pay[base + row * third : base + (row + 1) * third, col : col + v.shape[1]] = v

    fold_piece(put, lambda g, col, n: bo[g * third : (g + 1) * third, col : col + n], ocol)
    load_q.wait()
    units = hid[...].reshape(1, hid.shape[0])
    for j in range(PARTS):

        @pl.when(idx[0] == j)
        def _(j=j):
            pay[half + 2 : half + 3, 2 * hc :] = units[:, j * fc : (j + 1) * fc]
            for s in range(3):
                pay[:half, s * hc : (s + 1) * hc] = bq[
                    :, s * width + j * hc : s * width + (j + 1) * hc
                ]

    load_x.wait()


def pack2_kernel(idx, wup, wdown, pay, bu, sem):
    half = bu.shape[0]
    fc = pay.shape[0] - half
    units = wdown.shape[0]
    shards = wup.shape[1] // units
    fpart = units // PARTS
    load_u = pltpu.make_async_copy(wup.at[at(idx[1] * half, half, 32)], bu, sem.at[0])
    load_d = pltpu.make_async_copy(
        wdown.at[at(idx[0] * fpart + idx[1] * fc, fc, 32)], pay.at[half:], sem.at[1]
    )
    load_u.start()
    load_d.start()
    load_u.wait()
    for j in range(PARTS):

        @pl.when(idx[0] == j)
        def _(j=j):
            for s in range(shards):
                base = (s * PARTS + j) * fpart
                pay[:half, s * fpart : (s + 1) * fpart] = bu[:, base : base + fpart]

    load_d.wait()


def split_kernel(g0, g1, g2, g3, first, second):
    base = first.shape[1]
    cols = second.shape[2]
    third = second.shape[1] // 3
    for k, g in enumerate((g0, g1, g2, g3)):
        first[k] = g[:base, :]
        top, low = g[base : base + third, :], g[base + third :, :]
        second[k, :third] = top[:, :cols]
        second[k, third : 2 * third] = low[:, :cols]
        second[k, 2 * third :, : cols // 2] = top[:, cols:]
        second[k, 2 * third :, cols // 2 :] = low[:, cols:]


def sum_kernel(*refs):
    out = refs[-1]
    v = refs[0][...].astype(F32)
    for r in refs[1:-1]:
        v = v + r[...].astype(F32)
    out[...] = v.astype(out.dtype)


def wq_kernel(idx, mine, other, wq, small, bias):
    c, core, z = idx[0], idx[1], idx[2]
    shards, _, span = mine.shape
    hc = span // 3
    half = wq.shape[0] // shards // CORES
    for m in range(shards):
        base = (z ^ m) * (CORES * half)
        wq[at(base + core * half, half, 32), :] = mine[m, :half, :]
        wq[at(base + (1 - core) * half, half, 32), :] = other[m, :half, :]
    small[...] = jnp.zeros_like(small)
    for j in range(shards):
        e = mine[j ^ z, half:, :].astype(F32)
        for n in range(9):
            small[n : n + 1, j * hc : (j + 1) * hc] = e[
                n // 3 : n // 3 + 1, (n % 3) * hc : (n % 3 + 1) * hc
            ]
    e = mine[c ^ z, half:, :].astype(F32)[:1]
    row = jnp.concatenate([e[:, :hc], jnp.zeros((1, hc), F32), e[:, hc : 2 * hc]], axis=1)
    bias[...] = jnp.broadcast_to(row, bias.shape)


def attn_kernel(x, wq, bias, pj, probs, out):
    rows, span = pj.shape
    hc = span // 3
    heads = hc // HEAD_DIM
    scale = 1.0 / math.sqrt(HEAD_DIM)
    pj[...] = (mm(x[:rows, :], wq[...]) + bias[:1, :]).astype(BF)
    pos_r = lax.broadcasted_iota(jnp.int32, (rows, 1), 0).astype(F32)
    pos_c = lax.broadcasted_iota(jnp.int32, (1, rows), 1).astype(F32)
    lens = x[rows : rows + 16, :128].astype(F32)[:1]
    end = jnp.zeros((1, 1), F32)
    seg_r = jnp.zeros((rows, 1), F32)
    seg_c = jnp.zeros((1, rows), F32)
    for n in range(3):
        end = end + lens[:, n : n + 1]
        seg_r = seg_r + (pos_r >= end).astype(F32)
        seg_c = seg_c + (pos_c >= end).astype(F32)
    same = seg_r == seg_c
    pb = pj[...]
    mixes = []
    for h in range(heads):
        q = pb[:, h * HEAD_DIM : (h + 1) * HEAD_DIM]
        k = pb[:, hc + h * HEAD_DIM : hc + (h + 1) * HEAD_DIM]
        v = pb[:, 2 * hc + h * HEAD_DIM : 2 * hc + (h + 1) * HEAD_DIM]
        s = jnp.where(same, mm_tb(q, k) * scale, masked_score)
        e = jnp.exp(s - jnp.max(s, axis=-1, keepdims=True))
        p = e / jnp.sum(e, axis=-1, keepdims=True)
        probs[h] = p
        mixes.append(mm(p.astype(BF), v))
    out[...] = jnp.concatenate(mixes, axis=1).astype(BF)


def wo_kernel(idx, mine, other, wo):
    c, core, z = idx[0], idx[1], idx[2]
    parts, shards, piece, cols = mine.shape
    for k in range(parts):
        for m in range(shards):
            base = at((z ^ m) * (parts * piece) + (c ^ k) * piece, piece, 16)
            wo[base, at(core * cols, cols, 128)] = mine[k, m]
            wo[base, at((1 - core) * cols, cols, 128)] = other[k, m]


def out_kernel(idx, tok, m0, m1, m2, m3, wo, small, y1, y1low, unit, inv):
    c = idx[0]
    hc = m0.shape[1]
    acc = small[2:3, :]
    for k, m in enumerate((m0, m1, m2, m3)):
        acc = acc + mm(m[...], wo[at((c ^ k) * hc, hc, 64), :])
    u, r = norm_stats(tok[...].astype(F32) + acc)
    unit[...] = u
    inv[...] = jnp.broadcast_to(r, inv.shape)
    y = u * small[6:7, :] + small[3:4, :]
    y1[...] = y
    y1low[...] = y.astype(BF)


def join_kernel(near, far, out):
    out[:2] = near[...]
    out[2:] = far[...]


def stack_kernel(g0, g1, g2, g3, out):
    for k, g in enumerate((g0, g1, g2, g3)):
        out[k] = g[...]


def w2_kernel(idx, mine, other, wu, wd):
    core, z = idx[1], idx[2]
    half = mine.shape[1] // 2
    for m in range(mine.shape[0]):
        base = (z ^ m) * (2 * half)
        lo = at(base + core * half, half, 32)
        hi = at(base + (1 - core) * half, half, 32)
        wu[lo, :] = mine[m, :half, :]
        wu[hi, :] = other[m, :half, :]
        wd[lo, :] = mine[m, half:, :]
        wd[hi, :] = other[m, half:, :]


def ffn_kernel(y, wu, wd, small, act, slope, out):
    u = mm(y[...], wu[...]) + small[8:9, :]
    phi, slp = gelu_parts(u)
    a = (u * phi).astype(BF)
    act[...] = a
    slope[...] = slp
    out[...] = mm(a, wd[...]).astype(out.dtype)


def ln2_kernel(y1, z0, r1, r2, r3, small, cot, x0, actv, dz, gh2, sm):
    rows = y1.shape[0]
    branch = z0[...] + r1[...].astype(F32) + r2[...].astype(F32) + r3[...].astype(F32)
    u, r = norm_stats(y1[...] + (branch + small[4:5, :]))
    lens = x0[rows : rows + 16, :128].astype(F32)[:1]
    total = lens[:, 0:1] + lens[:, 1:2] + lens[:, 2:3]
    keep = (lax.broadcasted_iota(jnp.int32, (rows, 1), 0).astype(F32) < total).astype(F32)
    actv[...] = ((u * small[7:8, :] + small[5:6, :]) * keep).astype(BF)
    g = cot[...].astype(F32) * keep
    gh = norm_back(g, u, r, small[7:8, :])
    gh2[...] = gh
    low = gh.astype(BF)
    dz[...] = low
    sm[...] = jnp.zeros_like(sm)
    sm[0:1, :] = col_sum(low.astype(F32))
    sm[1:2, :] = col_sum(g)
    sm[2:3, :] = col_sum(g * u)


def ffb_kernel(d, wu, wd, slope, du, out):
    t = (mm_tb(d[...], wd[...]) * slope[...]).astype(BF)
    du[...] = t
    out[...] = mm_tb(t, wu[...]).astype(out.dtype)


def ffw_kernel(idx, *refs):
    core = idx[1]
    groups = [refs[n * PARTS : (n + 1) * PARTS] for n in range(4)]
    give, mine, hid, left, right, full = refs[4 * PARTS :]
    rows, width = groups[0][0].shape
    shards = give.shape[0]
    half = width // shards // CORES
    acts, dzs, ys, dus = groups
    h = None
    for base, lefts, rights in ((0, ys, dus), (half, acts, dzs)):
        for k in range(PARTS):
            left[k * rows : (k + 1) * rows, :] = lefts[k][...]
            right[k * rows : (k + 1) * rows, :] = rights[k][...]
        if base == 0:
            h = col_sum(right[...].astype(F32))
        full[...] = mm_ta(left[...], right[...]).astype(BF)
        for j in range(shards):
            mine[j, base : base + half, :] = full[at(j * 2 * half + core * half, half, 32), :]
            give[j, base : base + half, :] = full[
                at(j * 2 * half + (1 - core) * half, half, 32), :
            ]
    hid[...] = jnp.broadcast_to(h, hid.shape)


def add_kernel(idx, mine, got, own, near, far, send):
    z = idx[2]
    for k, out in enumerate((own, near, far, send)):
        out[...] = (mine[z ^ k].astype(F32) + got[z ^ k].astype(F32)).astype(out.dtype)


def fin1_kernel(idx, mine, other, gup, gdown, token):
    c, core = idx[0], idx[1]
    parts, _, width = mine.shape
    half = gup.shape[0] // 2
    fc = gdown.shape[0] // parts
    shards = gup.shape[1] // (parts * fc)
    for j in range(parts):
        k = j ^ c
        token[...] = jnp.zeros_like(token)
        for src, row in ((mine, core * half), (other, (1 - core) * half)):
            v = src[k, :half, :].astype(F32)
            for s in range(shards):
                base = (s * parts + j) * fc
                gup[at(row, half, 32), base : base + fc] = v[:, s * fc : (s + 1) * fc]
            gdown[at(j * fc + row, half, 32), :] = src[k, half : 2 * half, :].astype(F32)


def ln1b_kernel(idx, gh2, o0, r1, r2, r3, unit, inv, small, wo, gh1, da, m0, m1, m2, m3, sm):
    c = idx[0]
    hc = m0.shape[1]
    dy = gh2[...] + o0[...] + r1[...].astype(F32) + r2[...].astype(F32) + r3[...].astype(F32)
    u = unit[...]
    gh = norm_back(dy, u, inv[:, :1], small[6:7, :])
    gh1[...] = gh
    low = gh.astype(BF)
    da[...] = low
    for k, m in enumerate((m0, m1, m2, m3)):
        m[...] = mm_tb(low, wo[at((c ^ k) * hc, hc, 64), :]).astype(BF)
    sm[...] = jnp.zeros_like(sm)
    sm[0:1, :] = col_sum(low.astype(F32))
    sm[1:2, :] = col_sum(dy)
    sm[2:3, :] = col_sum(dy * u)


def outw_kernel(idx, m0, m1, m2, m3, da, give, mine):
    c, core = idx[0], idx[1]
    cols = give.shape[2]
    lo, hi = da[:, :cols], da[:, cols:]
    first = core == 0
    keep = jnp.where(first, lo.astype(F32), hi.astype(F32)).astype(BF)
    pass_on = jnp.where(first, hi.astype(F32), lo.astype(F32)).astype(BF)
    for k, m in enumerate((m0, m1, m2, m3)):
        mine[c ^ k] = mm_ta(m[...], keep).astype(BF)
        give[c ^ k] = mm_ta(m[...], pass_on).astype(BF)


def oadd_kernel(idx, mine, got, own, s1, s2, s3):
    c = idx[0]
    shards, piece = own.shape[0], own.shape[1]
    for k, out in enumerate((own, s1, s2, s3)):
        rng = at((c ^ k) * piece, piece, 16)
        for j in range(shards):
            v = mine[j, rng, :].astype(F32) + got[j, rng, :].astype(F32)
            out[j] = v.astype(out.dtype)


def attb_kernel(d, pj, probs, dp):
    rows, hc = d.shape
    heads = hc // HEAD_DIM
    scale = 1.0 / math.sqrt(HEAD_DIM)
    pb = pj[...]
    db = d[...]
    dqs, dks, dvs = [], [], []
    for h in range(heads):
        q = pb[:, h * HEAD_DIM : (h + 1) * HEAD_DIM]
        k = pb[:, hc + h * HEAD_DIM : hc + (h + 1) * HEAD_DIM]
        v = pb[:, 2 * hc + h * HEAD_DIM : 2 * hc + (h + 1) * HEAD_DIM]
        g = db[:, h * HEAD_DIM : (h + 1) * HEAD_DIM]
        p = probs[h]
        dvs.append(mm_ta(p.astype(BF), g))
        dpr = mm_tb(g, v)
        inner = jnp.sum(p * dpr, axis=-1, keepdims=True)
        ds = (p * (dpr - inner)).astype(BF)
        dqs.append(mm(ds, k) * scale)
        dks.append(mm_ta(ds, q) * scale)
    dp[...] = jnp.concatenate(dqs + dks + dvs, axis=1).astype(BF)


def dx_kernel(d0, d1, d2, d3, wq, o0, o1, o2, o3):
    for d, out in ((d0, o0), (d1, o1), (d2, o2), (d3, o3)):
        out[...] = mm_tb(d[...], wq[...]).astype(out.dtype)


def qw_kernel(idx, x0, x1, x2, x3, d0, d1, d2, d3, sm1, sm2, hid, give, mine, xg, dp, full):
    c, core = idx[0], idx[1]
    shards, _, span = give.shape
    rows = d0.shape[0]
    hc = span // 3
    half = xg.shape[1] // shards // CORES
    for k, (x, d) in enumerate(((x0, d0), (x1, d1), (x2, d2), (x3, d3))):
        xg[k * rows : (k + 1) * rows, :] = x[:rows, :]
        dp[k * rows : (k + 1) * rows, :] = d[...]
    full[...] = mm_ta(xg[...], dp[...]).astype(BF)
    cols = col_sum(dp[...].astype(F32))
    vecs = (sm1[0:1], sm1[1:2], sm2[0:1], sm2[1:2], sm1[2:3], sm2[2:3])
    for j in range(shards):
        mine[j, :half, :] = full[at(j * 2 * half + core * half, half, 32), :]
        give[j, :half, :] = full[at(j * 2 * half + (1 - core) * half, half, 32), :]
        part = [v[:, j * hc : (j + 1) * hc] for v in vecs]
        own = jnp.where(c == j, 1.0, 0.0)
        rows = jnp.concatenate(
            [
                jnp.concatenate([cols[:, :hc] * own, cols[:, 2 * hc :] * own, part[0]], axis=1),
                jnp.concatenate(part[1:4], axis=1),
                jnp.concatenate(part[4:6] + [hid[:1, j * hc : (j + 1) * hc]], axis=1),
                jnp.zeros((13, span), F32),
            ],
            axis=0,
        ).astype(BF)
        mine[j, half:, :] = rows
        give[j, half:, :] = rows


def add2_kernel(idx, mine, got, osum, own, near, far, send):
    z = idx[2]
    base, _ = mine.shape[1:]
    piece, cols = osum.shape[1:]
    third = piece // 3
    for n, out in enumerate((own, near, far, send)):
        j = z ^ n
        out[:base, :] = (mine[j].astype(F32) + got[j].astype(F32)).astype(out.dtype)
        w = osum[j]

        def put(row, col, v, out=out):
            rng = slice(base + row * third, base + (row + 1) * third)
            out[rng, col : col + v.shape[1]] = v.astype(out.dtype)

        fold_piece(put, lambda g, col, k, w=w: w[g * third : (g + 1) * third, col : col + k], cols)


def fin2_kernel(idx, mine, other, gqkv, gout, gvec, ggain, ghid):
    c, core = idx[0], idx[1]
    parts, _, span = mine.shape
    hc = span // 3
    half = gqkv.shape[0] // 2
    width = gout.shape[1]
    piece = gout.shape[0] // parts
    cols = width // 2
    base = half + 16
    tot = mine[0, half:base, :].astype(F32)
    for k in range(1, parts):
        tot = tot + mine[k, half:base, :].astype(F32)
    for n in range(8):
        v = tot[n // 3 : n // 3 + 1, (n % 3) * hc : (n % 3 + 1) * hc]
        if n < 6:
            gvec[n : n + 1, :] = v
        else:
            ggain[n - 6 : n - 5, :] = v
    units = []
    for j in range(parts):
        k = j ^ c
        units.append(mine[k, half:base, :].astype(F32)[2:3, 2 * hc :])
        for src, who in ((mine, core), (other, 1 - core)):
            v = src[k, :half, :].astype(F32)
            for s in range(3):
                gqkv[at(who * half, half, 32), s * width + j * hc : s * width + (j + 1) * hc] = v[
                    :, s * hc : (s + 1) * hc
                ]
            w = src[k, base:, :].astype(F32)
            third = piece // 3
            last = jnp.concatenate([w[:third, cols:], w[third:, cols:]], axis=1)
            for g, v in enumerate((w[:third, :cols], w[third:, :cols], last)):
                row = j * piece + g * third
                gout[row : row + third, at(who * cols, cols, 128)] = v
    ghid[...] = jnp.concatenate(units, axis=1).reshape(ghid.shape)


def call(kernel, out, *args, idx=None, scratch=(), hbm=(), after=(), limit=VMEM_BYTES):
    shapes = [jax.ShapeDtypeStruct(s, d) for s, d in out]
    specs = [
        pl.BlockSpec(memory_space=pltpu.HBM if n in hbm else pltpu.VMEM) for n in range(len(args))
    ]
    args = args + tuple(after)
    specs = specs + [pl.BlockSpec(memory_space=pl.ANY) for _ in after]
    skip = len(args) + (idx is not None)
    drop = len(after)

    def run(*refs):
        kernel(*refs[: skip - drop], *refs[skip:])

    if idx is not None:
        specs = [pl.BlockSpec(memory_space=pltpu.SMEM)] + specs
        args = (idx,) + args
    return pl.pallas_call(
        run if drop else kernel,
        out_shape=shapes,
        in_specs=specs,
        out_specs=[pl.BlockSpec(memory_space=pltpu.VMEM) for _ in shapes],
        scratch_shapes=[pltpu.VMEM(*s) if isinstance(s, tuple) else s for s in scratch],
        compiler_params=pltpu.CompilerParams(vmem_limit_bytes=limit),
        name=kernel.__name__,
        cost_estimate=pl.CostEstimate(flops=COST, bytes_accessed=100000, transcendentals=0),
    )(*args)


def gate(x, after):
    n = len(after)
    return pl.pallas_call(
        lambda *refs: None,
        out_shape=jax.ShapeDtypeStruct(x.shape, x.dtype),
        in_specs=[pl.BlockSpec(memory_space=pl.ANY)] * (n + 1),
        out_specs=pl.BlockSpec(memory_space=pl.ANY),
        input_output_aliases={0: 0},
        compiler_params=pltpu.CompilerParams(vmem_limit_bytes=VMEM_BYTES),
        name="gate_kernel",
    )(x, *after)


def make_body(reps, shards):
    def xor_perm(n, k):
        return [(i, i ^ k) for i in range(n)]

    def swap_core(v):
        return lax.ppermute(v, "rep", xor_perm(reps, 1))

    def swap_part(v, k):
        return lax.ppermute(v, "rep", xor_perm(reps, CORES * k))

    def swap_shard(v, k):
        return lax.ppermute(v, "shard", xor_perm(shards, k))

    def spread_part(v):
        return [v] + [swap_part(v, k) for k in range(1, PARTS)]

    def spread_shard(v):
        return [v] + [swap_shard(v, k) for k in range(1, shards)]

    def relay_shard(v, after=None):
        near, far = swap_shard(v, 1), swap_shard(v, 2)
        if after is not None:
            far = gate(far, after(near))
        return [v, near, far, swap_shard(far, 1)]

    def trade_part(slots):
        return [slots[0]] + [swap_part(slots[k], k) for k in range(1, PARTS)]

    def trade_shard(slots):
        return [slots[0]] + [swap_shard(slots[k], k) for k in range(1, shards)]

    def total(slots):
        acc = slots[0]
        for s in slots[1:]:
            acc = acc + s.astype(F32)
        return acc

    def sum_outer(v):
        step = CORES * PARTS
        while step < reps:
            v = v + lax.ppermute(v, "rep", xor_perm(reps, step))
            step *= 2
        return v

    def body(
        tokens, w_qkv, w_out, w_up, w_down, vec_bias, ln_gain, hidden_bias, seq_lengths, cotangent
    ):
        rows, width = tokens.shape
        hid_own = hidden_bias.shape[0]
        wsh = width // shards
        half = wsh // CORES
        hc = width // PARTS
        fc = hid_own // PARTS
        span = 3 * hc
        piece = wsh // PARTS
        ocol = width // CORES
        rep = lax.axis_index("rep")
        z = lax.axis_index("shard")
        core = rep % CORES
        c = (rep // CORES) % PARTS
        idx = jnp.stack([c, core, z]).astype(jnp.int32)
        mats = [((rows, width), BF)]

        xp, pay1 = call(
            pack_kernel,
            [((rows + 16, width), BF), ((half + 16 + 2 * piece // 3, span), BF)],
            tokens,
            w_qkv,
            w_out,
            vec_bias,
            ln_gain,
            hidden_bias,
            seq_lengths,
            idx=idx,
            hbm=range(7),
            limit=PACK_BYTES,
            scratch=[
                ((half, 3 * width), BF),
                ((piece, ocol), BF),
                (vec_bias.shape, BF),
                (ln_gain.shape, BF),
                ((hid_own,), BF),
                (seq_lengths.shape, jnp.int32),
                pltpu.SemaphoreType.DMA((7,)),
            ],
        )
        xs = spread_part(xp)
        got1 = relay_shard(pay1, lambda near: [xs[3]])
        (pay2,) = call(
            pack2_kernel,
            [((half + fc // CORES, width), BF)],
            w_up,
            w_down,
            idx=idx,
            hbm=(0, 1),
            after=[xp],
            scratch=[((half, w_up.shape[1]), BF), pltpu.SemaphoreType.DMA((2,))],
        )
        pay2 = gate(pay2, [got1[3]] + xs[1:])
        mine1, pay_o = call(
            split_kernel,
            [((shards, half + 16, span), BF), ((shards, piece, ocol), BF)],
            *got1,
        )
        other1 = swap_core(mine1)
        pair_o = jnp.stack([pay_o, swap_part(pay_o, 1)])
        far_o = swap_part(pair_o, 2)

        wq, small, bias = call(
            wq_kernel,
            [((width, span), BF), ((16, width), F32), ((8, span), F32)],
            mine1,
            other1,
            idx=idx,
            after=[pay2],
        )
        att = [
            call(
                attn_kernel,
                [((rows, span), BF), ((HEADS // PARTS, rows, rows), F32), ((rows, hc), BF)],
                x,
                wq,
                bias,
            )
            for k, x in enumerate(xs)
        ]
        mix = trade_part([a[2] for a in att])
        got2 = relay_shard(pay2, lambda near: mix[1:] + [near])
        (mine_o,) = call(
            join_kernel, [((PARTS,) + pay_o.shape, BF)], pair_o, far_o, after=[att[3][2]]
        )
        other_o = swap_core(mine_o)
        (wo,) = call(wo_kernel, [((width, width), BF)], mine_o, other_o, idx=idx)
        y1, y1low, unit1, inv1 = call(
            out_kernel,
            [((rows, width), F32), ((rows, width), BF), ((rows, width), F32), ((rows, 128), F32)],
            tokens,
            *mix,
            wo,
            small,
            idx=idx,
        )
        ys = spread_part(y1low)
        (mine2,) = call(
            stack_kernel, [((shards,) + pay2.shape, BF)], *got2, after=ys[1:]
        )
        wu, wd = call(
            w2_kernel,
            [((width, shards * fc), BF), ((shards * fc, width), BF)],
            mine2,
            swap_core(mine2),
            idx=idx,
        )
        part_type = [F32] + [BF] * (PARTS - 1)
        ffn = [
            call(
                ffn_kernel,
                [((rows, shards * fc), BF), ((rows, shards * fc), F32), ((rows, width), t)],
                y,
                wu,
                wd,
                small,
            )
            for y, t in zip(ys, part_type)
        ]
        activations, dz, gh2, sm2 = call(
            ln2_kernel,
            mats * 2 + [((rows, width), F32), ((8, width), F32)],
            y1,
            *trade_part([f[2] for f in ffn]),
            small,
            cotangent,
            xp,
        )
        dzs = spread_part(dz)
        ffb = [
            call(
                ffb_kernel, [((rows, shards * fc), BF), ((rows, width), t)], d, wu, wd, f[1]
            )
            for d, f, t in list(zip(dzs, ffn, part_type))[1:]
        ]
        ffb = [
            call(
                ffb_kernel,
                [((rows, shards * fc), BF), ((rows, width), F32)],
                dz,
                wu,
                wd,
                ffn[0][1],
                after=[f[0] for f in ffb],
            )
        ] + ffb
        dyp = trade_part([f[1] for f in ffb])
        rows1 = half + fc // CORES
        give1, keep1, sm3 = call(
            ffw_kernel,
            [((shards, rows1, width), BF)] * 2 + [((8, shards * fc), F32)],
            *[f[0] for f in ffn],
            *dzs,
            *ys,
            *[f[0] for f in ffb],
            idx=idx,
            after=[dyp[3]],
            scratch=[((PARTS * rows, width), BF)] * 2 + [((width, width), BF)],
        )
        def relay_sum(far, send, after):
            got = swap_shard(send, 1)
            (low,) = call(sum_kernel, [(far.shape, BF)], far, got, after=after)
            return low, swap_shard(low, 2)

        def join(own, near, far, after):
            if reps > CORES * PARTS:
                return sum_outer(own + near.astype(F32) + far.astype(F32)).astype(BF)
            return call(sum_kernel, [(own.shape, BF)], own, near, far, after=after)[0]

        def spread_piece(v, after):
            (done,) = call(
                stack_kernel, [((PARTS,) + v.shape, BF)], *spread_part(v), after=after
            )
            return done, swap_core(done)

        def pair_shapes(n, w):
            return [((n, w), F32), ((n, w), BF), ((n, w), F32), ((n, w), BF)]

        own_a, near_a, far_a, send_a = call(
            add_kernel,
            pair_shapes(rows1, width),
            keep1,
            swap_core(give1),
            idx=idx,
            after=[dyp[3]],
        )
        gh1, da, *rest = call(
            ln1b_kernel,
            [((rows, width), F32)] + mats + [((rows, hc), BF)] * PARTS + [((8, width), F32)],
            gh2,
            *dyp,
            unit1,
            inv1,
            small,
            wo,
            idx=idx,
            after=[send_a],
        )
        dm, sm1 = trade_part(rest[:PARTS]), rest[PARTS]
        give_o, keep_o = call(
            outw_kernel,
            [((shards, wsh, ocol), BF)] * 2,
            *mix,
            da,
            idx=idx,
            after=[sm1],
        )
        out_send = call(
            oadd_kernel,
            [((shards, piece, ocol), F32)] + [((shards, piece, ocol), BF)] * 3,
            keep_o,
            swap_core(give_o),
            idx=idx,
        )
        out_got = trade_part(out_send)
        osum = total(out_got)

        dps = [
            call(
                attb_kernel,
                [((rows, span), BF)],
                d,
                a[0],
                a[1],
                after=[out_send[0]] if k < 2 else [],
            )[0]
            for k, (d, a) in enumerate(zip(dm, att))
        ]
        low_a, got_a = relay_sum(far_a, send_a, [dps[3]])
        near_a = swap_shard(gate(near_a, [low_a]), 1)
        rows2 = half + 16
        give2, keep2 = call(
            qw_kernel,
            [((shards, rows2, span), BF)] * 2,
            *xs,
            *dps,
            sm1,
            sm2,
            sm3,
            idx=idx,
            after=[out_got[1], low_a],
            scratch=[
                ((PARTS * rows, width), BF),
                ((PARTS * rows, span), BF),
                ((width, span), BF),
            ],
        )
        dxp = call(
            dx_kernel, [((rows, width), t) for t in part_type], *dps, wq, after=[give2] + out_got[2:]
        )
        dxp_got = trade_part(dxp)
        own_b, near_b, far_b, send_b = call(
            add2_kernel,
            pair_shapes(rows2 + 2 * piece // 3, span),
            keep2,
            swap_core(give2),
            osum,
            idx=idx,
            after=[got_a, near_a, dxp[0]],
        )
        low_b, got_b = relay_sum(far_b, send_b, dxp_got[1:])
        near_b = swap_shard(gate(near_b, [low_b]), 1)
        piece1 = join(own_a, near_a, got_a, [low_b])
        done1 = spread_piece(piece1, [got_b, near_b])
        piece2 = join(own_b, near_b, got_b, [])
        done2 = spread_piece(piece2, [])
        g_tok = gh1 + total(dxp_got)
        gw_up, gw_down, token = call(
            fin1_kernel, [(w_up.shape, F32), (w_down.shape, F32), ((8, 128), F32)], *done1, idx=idx, after=[piece2]
        )
        gw_qkv, gw_out, g_vec, g_gain, g_hidden = call(
            fin2_kernel,
            [
                (w_qkv.shape, F32),
                (w_out.shape, F32),
                ((6, wsh), F32),
                ((2, wsh), F32),
                ((hid_own,), F32),
            ],
            *done2,
            idx=idx,
            after=[token, g_tok],
        )
        return (
            activations,
            g_tok,
            gw_qkv,
            gw_out,
            gw_up,
            gw_down,
            g_vec,
            g_gain,
            g_hidden,
        )

    return body


def solution(mesh):
    body = make_body(mesh.shape["rep"], mesh.shape["shard"])
    both = P(("rep", "shard"), None)
    first = P("shard", None)
    last = P(None, "shard")
    return jax.shard_map(
        body,
        mesh=mesh,
        in_specs=(both, first, first, first, first, last, last, P("shard"), both, both),
        out_specs=(both, both, first, first, first, first, last, last, P("shard")),
        check_vma=False,
    )
```

```python
import functools
import math

import jax
import jax.numpy as jnp
from jax import lax
from jax.experimental import pallas as pl
from jax.experimental.pallas import tpu as pltpu
from jax.sharding import PartitionSpec as P

HEADS = 12
HEAD_DIM = 64
PARTS = 4
CORES = 2
layer_eps = 1e-12
masked_score = -1000000000.0
BF = jnp.bfloat16
F32 = jnp.float32
VMEM_BYTES = 48 * 1024 * 1024
PACK_BYTES = 62 * 1024 * 1024
COST = 11 * 10**9


def mm(a, b):
    return jnp.dot(a, b, preferred_element_type=F32)


def mm_ta(a, b):
    return lax.dot_general(a, b, (((0,), (0,)), ((), ())), preferred_element_type=F32)


def mm_tb(a, b):
    return lax.dot_general(a, b, (((1,), (1,)), ((), ())), preferred_element_type=F32)


def at(start, size, unit):
    return pl.ds(pl.multiple_of(start, unit), size)


def norm_stats(h):
    centre = h - jnp.mean(h, axis=-1, keepdims=True)
    inv = lax.rsqrt(jnp.mean(centre * centre, axis=-1, keepdims=True) + layer_eps)
    return centre * inv, inv


def norm_back(g, unit, inv, gain):
    gg = g * gain
    m1 = jnp.mean(gg, axis=-1, keepdims=True)
    m2 = jnp.mean(gg * unit, axis=-1, keepdims=True)
    return inv * (gg - m1 - unit * m2)


def gelu_parts(u):
    phi = 0.5 * (1.0 + lax.erf(u * (1.0 / math.sqrt(2.0))))
    dens = jnp.exp(-0.5 * u * u) * (1.0 / math.sqrt(2.0 * math.pi))
    return phi, phi + u * dens


def col_sum(v):
    return jnp.sum(v, axis=0, keepdims=True)


def fold_piece(put, get, cols):
    put(0, 0, get(0, 0, cols))
    put(1, 0, get(1, 0, cols))
    put(0, cols, get(2, 0, cols // 2))
    put(1, cols, get(2, cols // 2, cols // 2))


def pack_kernel(idx, tok, wqkv, wout, vec_in, gain_in, hid_in, lens_in, xp, pay, bq, bo, vec, gain, hid, lens, sem):
    rows, width = tok.shape
    half = bq.shape[0]
    piece, ocol = bo.shape
    hc = width // PARTS
    fc = hid.shape[0] // PARTS
    load_q = pltpu.make_async_copy(wqkv.at[at(idx[1] * half, half, 32)], bq, sem.at[0])
    load_o = pltpu.make_async_copy(
        wout.at[at(idx[0] * piece, piece, 16), at(idx[1] * ocol, ocol, 128)], bo, sem.at[1]
    )
    load_x = pltpu.make_async_copy(tok, xp.at[:rows], sem.at[2])
    small = [
        pltpu.make_async_copy(a, b, sem.at[3 + n])
        for n, (a, b) in enumerate(
            ((vec_in, vec), (gain_in, gain), (hid_in, hid), (lens_in, lens))
        )
    ]
    load_q.start()
    load_x.start()
    load_o.start()
    for load in small:
        load.start()
    base = half + 16
    pay[half:base] = jnp.zeros((16, 3 * hc), BF)
    xp[rows:] = jnp.zeros((16, width), BF)
    for load in small:
        load.wait()
    xp[rows : rows + 1, : lens.shape[1]] = lens[...].astype(BF)
    for n in range(8):
        src = vec[n : n + 1, :] if n < 6 else gain[n - 6 : n - 5, :]
        pay[half + n // 3 : half + n // 3 + 1, (n % 3) * hc : (n % 3 + 1) * hc] = src
    load_o.wait()
    third = piece // 3

    def put(row, col, v):
        pay[base + row * third : base + (row + 1) * third, col : col + v.shape[1]] = v

    fold_piece(put, lambda g, col, n: bo[g * third : (g + 1) * third, col : col + n], ocol)
    load_q.wait()
    units = hid[...].reshape(1, hid.shape[0])
    for j in range(PARTS):

        @pl.when(idx[0] == j)
        def _(j=j):
            pay[half + 2 : half + 3, 2 * hc :] = units[:, j * fc : (j + 1) * fc]
            for s in range(3):
                pay[:half, s * hc : (s + 1) * hc] = bq[
                    :, s * width + j * hc : s * width + (j + 1) * hc
                ]

    load_x.wait()


def pack2_kernel(idx, wup, wdown, pay, bu, sem):
    half = bu.shape[0]
    fc = pay.shape[0] - half
    units = wdown.shape[0]
    shards = wup.shape[1] // units
    fpart = units // PARTS
    load_u = pltpu.make_async_copy(wup.at[at(idx[1] * half, half, 32)], bu, sem.at[0])
    load_d = pltpu.make_async_copy(
        wdown.at[at(idx[0] * fpart + idx[1] * fc, fc, 32)], pay.at[half:], sem.at[1]
    )
    load_u.start()
    load_d.start()
    load_u.wait()
    for j in range(PARTS):

        @pl.when(idx[0] == j)
        def _(j=j):
            for s in range(shards):
                base = (s * PARTS + j) * fpart
                pay[:half, s * fpart : (s + 1) * fpart] = bu[:, base : base + fpart]

    load_d.wait()


def split_kernel(g0, g1, g2, g3, first, second):
    base = first.shape[1]
    cols = second.shape[2]
    third = second.shape[1] // 3
    for k, g in enumerate((g0, g1, g2, g3)):
        first[k] = g[:base, :]
        top, low = g[base : base + third, :], g[base + third :, :]
        second[k, :third] = top[:, :cols]
        second[k, third : 2 * third] = low[:, :cols]
        second[k, 2 * third :, : cols // 2] = top[:, cols:]
        second[k, 2 * third :, cols // 2 :] = low[:, cols:]


def sum_kernel(*refs):
    out = refs[-1]
    v = refs[0][...].astype(F32)
    for r in refs[1:-1]:
        v = v + r[...].astype(F32)
    out[...] = v.astype(out.dtype)


def wq_kernel(idx, mine, other, wq, small, bias):
    c, core, z = idx[0], idx[1], idx[2]
    shards, _, span = mine.shape
    hc = span // 3
    half = wq.shape[0] // shards // CORES
    for m in range(shards):
        base = (z ^ m) * (CORES * half)
        wq[at(base + core * half, half, 32), :] = mine[m, :half, :]
        wq[at(base + (1 - core) * half, half, 32), :] = other[m, :half, :]
    small[...] = jnp.zeros_like(small)
    for j in range(shards):
        e = mine[j ^ z, half:, :].astype(F32)
        for n in range(9):
            small[n : n + 1, j * hc : (j + 1) * hc] = e[
                n // 3 : n // 3 + 1, (n % 3) * hc : (n % 3 + 1) * hc
            ]
    e = mine[c ^ z, half:, :].astype(F32)[:1]
    row = jnp.concatenate([e[:, :hc], jnp.zeros((1, hc), F32), e[:, hc : 2 * hc]], axis=1)
    bias[...] = jnp.broadcast_to(row, bias.shape)


def attn_kernel(x, wq, bias, pj, probs, out):
    rows, span = pj.shape
    hc = span // 3
    heads = hc // HEAD_DIM
    scale = 1.0 / math.sqrt(HEAD_DIM)
    pj[...] = (mm(x[:rows, :], wq[...]) + bias[:1, :]).astype(BF)
    pos_r = lax.broadcasted_iota(jnp.int32, (rows, 1), 0).astype(F32)
    pos_c = lax.broadcasted_iota(jnp.int32, (1, rows), 1).astype(F32)
    lens = x[rows : rows + 16, :128].astype(F32)[:1]
    end = jnp.zeros((1, 1), F32)
    seg_r = jnp.zeros((rows, 1), F32)
    seg_c = jnp.zeros((1, rows), F32)
    for n in range(3):
        end = end + lens[:, n : n + 1]
        seg_r = seg_r + (pos_r >= end).astype(F32)
        seg_c = seg_c + (pos_c >= end).astype(F32)
    same = seg_r == seg_c
    pb = pj[...]
    mixes = []
    for h in range(heads):
        q = pb[:, h * HEAD_DIM : (h + 1) * HEAD_DIM]
        k = pb[:, hc + h * HEAD_DIM : hc + (h + 1) * HEAD_DIM]
        v = pb[:, 2 * hc + h * HEAD_DIM : 2 * hc + (h + 1) * HEAD_DIM]
        s = jnp.where(same, mm_tb(q, k) * scale, masked_score)
        e = jnp.exp(s - jnp.max(s, axis=-1, keepdims=True))
        p = e / jnp.sum(e, axis=-1, keepdims=True)
        probs[h] = p
        mixes.append(mm(p.astype(BF), v))
    out[...] = jnp.concatenate(mixes, axis=1).astype(BF)


def wo_kernel(idx, mine, other, wo):
    c, core, z = idx[0], idx[1], idx[2]
    parts, shards, piece, cols = mine.shape
    for k in range(parts):
        for m in range(shards):
            base = at((z ^ m) * (parts * piece) + (c ^ k) * piece, piece, 16)
            wo[base, at(core * cols, cols, 128)] = mine[k, m]
            wo[base, at((1 - core) * cols, cols, 128)] = other[k, m]


def out_kernel(idx, tok, m0, m1, m2, m3, wo, small, y1, y1low, unit, inv):
    c = idx[0]
    hc = m0.shape[1]
    acc = small[2:3, :]
    for k, m in enumerate((m0, m1, m2, m3)):
        acc = acc + mm(m[...], wo[at((c ^ k) * hc, hc, 64), :])
    u, r = norm_stats(tok[...].astype(F32) + acc)
    unit[...] = u
    inv[...] = jnp.broadcast_to(r, inv.shape)
    y = u * small[6:7, :] + small[3:4, :]
    y1[...] = y
    y1low[...] = y.astype(BF)


def join_kernel(near, far, out):
    out[:2] = near[...]
    out[2:] = far[...]


def stack_kernel(g0, g1, g2, g3, out):
    for k, g in enumerate((g0, g1, g2, g3)):
        out[k] = g[...]


def w2_kernel(idx, mine, other, wu, wd):
    core, z = idx[1], idx[2]
    half = mine.shape[1] // 2
    for m in range(mine.shape[0]):
        base = (z ^ m) * (2 * half)
        lo = at(base + core * half, half, 32)
        hi = at(base + (1 - core) * half, half, 32)
        wu[lo, :] = mine[m, :half, :]
        wu[hi, :] = other[m, :half, :]
        wd[lo, :] = mine[m, half:, :]
        wd[hi, :] = other[m, half:, :]


def ffn_kernel(y, wu, wd, small, act, slope, out):
    u = mm(y[...], wu[...]) + small[8:9, :]
    phi, slp = gelu_parts(u)
    a = (u * phi).astype(BF)
    act[...] = a
    slope[...] = slp
    out[...] = mm(a, wd[...]).astype(out.dtype)


def ln2_kernel(y1, z0, r1, r2, r3, small, cot, x0, actv, dz, gh2, sm):
    rows = y1.shape[0]
    branch = z0[...] + r1[...].astype(F32) + r2[...].astype(F32) + r3[...].astype(F32)
    u, r = norm_stats(y1[...] + (branch + small[4:5, :]))
    lens = x0[rows : rows + 16, :128].astype(F32)[:1]
    total = lens[:, 0:1] + lens[:, 1:2] + lens[:, 2:3]
    keep = (lax.broadcasted_iota(jnp.int32, (rows, 1), 0).astype(F32) < total).astype(F32)
    actv[...] = ((u * small[7:8, :] + small[5:6, :]) * keep).astype(BF)
    g = cot[...].astype(F32) * keep
    gh = norm_back(g, u, r, small[7:8, :])
    gh2[...] = gh
    low = gh.astype(BF)
    dz[...] = low
    sm[...] = jnp.zeros_like(sm)
    sm[0:1, :] = col_sum(low.astype(F32))
    sm[1:2, :] = col_sum(g)
    sm[2:3, :] = col_sum(g * u)


def ffb_kernel(d, wu, wd, slope, du, out):
    t = (mm_tb(d[...], wd[...]) * slope[...]).astype(BF)
    du[...] = t
    out[...] = mm_tb(t, wu[...]).astype(out.dtype)


def ffw_kernel(idx, *refs):
    core = idx[1]
    groups = [refs[n * PARTS : (n + 1) * PARTS] for n in range(4)]
    give, mine, hid, left, right, full = refs[4 * PARTS :]
    rows, width = groups[0][0].shape
    shards = give.shape[0]
    half = width // shards // CORES
    acts, dzs, ys, dus = groups
    h = None
    for base, lefts, rights in ((0, ys, dus), (half, acts, dzs)):
        for k in range(PARTS):
            left[k * rows : (k + 1) * rows, :] = lefts[k][...]
            right[k * rows : (k + 1) * rows, :] = rights[k][...]
        if base == 0:
            h = col_sum(right[...].astype(F32))
        full[...] = mm_ta(left[...], right[...]).astype(BF)
        for j in range(shards):
            mine[j, base : base + half, :] = full[at(j * 2 * half + core * half, half, 32), :]
            give[j, base : base + half, :] = full[
                at(j * 2 * half + (1 - core) * half, half, 32), :
            ]
    hid[...] = jnp.broadcast_to(h, hid.shape)


def add_kernel(idx, mine, got, own, near, far, send):
    z = idx[2]
    for k, out in enumerate((own, near, far, send)):
        out[...] = (mine[z ^ k].astype(F32) + got[z ^ k].astype(F32)).astype(out.dtype)


def fin1_kernel(idx, mine, other, gup, gdown, token):
    c, core = idx[0], idx[1]
    parts, _, width = mine.shape
    half = gup.shape[0] // 2
    fc = gdown.shape[0] // parts
    shards = gup.shape[1] // (parts * fc)
    for j in range(parts):
        k = j ^ c
        token[...] = jnp.zeros_like(token)
        for src, row in ((mine, core * half), (other, (1 - core) * half)):
            v = src[k, :half, :].astype(F32)
            for s in range(shards):
                base = (s * parts + j) * fc
                gup[at(row, half, 32), base : base + fc] = v[:, s * fc : (s + 1) * fc]
            gdown[at(j * fc + row, half, 32), :] = src[k, half : 2 * half, :].astype(F32)


def ln1b_kernel(idx, gh2, o0, r1, r2, r3, unit, inv, small, wo, gh1, da, m0, m1, m2, m3, sm):
    c = idx[0]
    hc = m0.shape[1]
    dy = gh2[...] + o0[...] + r1[...].astype(F32) + r2[...].astype(F32) + r3[...].astype(F32)
    u = unit[...]
    gh = norm_back(dy, u, inv[:, :1], small[6:7, :])
    gh1[...] = gh
    low = gh.astype(BF)
    da[...] = low
    for k, m in enumerate((m0, m1, m2, m3)):
        m[...] = mm_tb(low, wo[at((c ^ k) * hc, hc, 64), :]).astype(BF)
    sm[...] = jnp.zeros_like(sm)
    sm[0:1, :] = col_sum(low.astype(F32))
    sm[1:2, :] = col_sum(dy)
    sm[2:3, :] = col_sum(dy * u)


def outw_kernel(idx, m0, m1, m2, m3, da, give, mine):
    c, core = idx[0], idx[1]
    cols = give.shape[2]
    lo, hi = da[:, :cols], da[:, cols:]
    first = core == 0
    keep = jnp.where(first, lo.astype(F32), hi.astype(F32)).astype(BF)
    pass_on = jnp.where(first, hi.astype(F32), lo.astype(F32)).astype(BF)
    for k, m in enumerate((m0, m1, m2, m3)):
        mine[c ^ k] = mm_ta(m[...], keep).astype(BF)
        give[c ^ k] = mm_ta(m[...], pass_on).astype(BF)


def oadd_kernel(idx, mine, got, own, s1, s2, s3):
    c = idx[0]
    shards, piece = own.shape[0], own.shape[1]
    for k, out in enumerate((own, s1, s2, s3)):
        rng = at((c ^ k) * piece, piece, 16)
        for j in range(shards):
            v = mine[j, rng, :].astype(F32) + got[j, rng, :].astype(F32)
            out[j] = v.astype(out.dtype)


def attb_kernel(d, pj, probs, dp):
    rows, hc = d.shape
    heads = hc // HEAD_DIM
    scale = 1.0 / math.sqrt(HEAD_DIM)
    pb = pj[...]
    db = d[...]
    dqs, dks, dvs = [], [], []
    for h in range(heads):
        q = pb[:, h * HEAD_DIM : (h + 1) * HEAD_DIM]
        k = pb[:, hc + h * HEAD_DIM : hc + (h + 1) * HEAD_DIM]
        v = pb[:, 2 * hc + h * HEAD_DIM : 2 * hc + (h + 1) * HEAD_DIM]
        g = db[:, h * HEAD_DIM : (h + 1) * HEAD_DIM]
        p = probs[h]
        dvs.append(mm_ta(p.astype(BF), g))
        dpr = mm_tb(g, v)
        inner = jnp.sum(p * dpr, axis=-1, keepdims=True)
        ds = (p * (dpr - inner)).astype(BF)
        dqs.append(mm(ds, k) * scale)
        dks.append(mm_ta(ds, q) * scale)
    dp[...] = jnp.concatenate(dqs + dks + dvs, axis=1).astype(BF)


def dx_kernel(d0, d1, d2, d3, wq, o0, o1, o2, o3):
    for d, out in ((d0, o0), (d1, o1), (d2, o2), (d3, o3)):
        out[...] = mm_tb(d[...], wq[...]).astype(out.dtype)


def qw_kernel(idx, x0, x1, x2, x3, d0, d1, d2, d3, sm1, sm2, hid, give, mine, xg, dp, full):
    c, core = idx[0], idx[1]
    shards, _, span = give.shape
    rows = d0.shape[0]
    hc = span // 3
    half = xg.shape[1] // shards // CORES
    for k, (x, d) in enumerate(((x0, d0), (x1, d1), (x2, d2), (x3, d3))):
        xg[k * rows : (k + 1) * rows, :] = x[:rows, :]
        dp[k * rows : (k + 1) * rows, :] = d[...]
    full[...] = mm_ta(xg[...], dp[...]).astype(BF)
    cols = col_sum(dp[...].astype(F32))
    vecs = (sm1[0:1], sm1[1:2], sm2[0:1], sm2[1:2], sm1[2:3], sm2[2:3])
    for j in range(shards):
        mine[j, :half, :] = full[at(j * 2 * half + core * half, half, 32), :]
        give[j, :half, :] = full[at(j * 2 * half + (1 - core) * half, half, 32), :]
        part = [v[:, j * hc : (j + 1) * hc] for v in vecs]
        own = jnp.where(c == j, 1.0, 0.0)
        rows = jnp.concatenate(
            [
                jnp.concatenate([cols[:, :hc] * own, cols[:, 2 * hc :] * own, part[0]], axis=1),
                jnp.concatenate(part[1:4], axis=1),
                jnp.concatenate(part[4:6] + [hid[:1, j * hc : (j + 1) * hc]], axis=1),
                jnp.zeros((13, span), F32),
            ],
            axis=0,
        ).astype(BF)
        mine[j, half:, :] = rows
        give[j, half:, :] = rows


def add2_kernel(idx, mine, got, osum, own, near, far, send):
    z = idx[2]
    base, _ = mine.shape[1:]
    piece, cols = osum.shape[1:]
    third = piece // 3
    for n, out in enumerate((own, near, far, send)):
        j = z ^ n
        out[:base, :] = (mine[j].astype(F32) + got[j].astype(F32)).astype(out.dtype)
        w = osum[j]

        def put(row, col, v, out=out):
            rng = slice(base + row * third, base + (row + 1) * third)
            out[rng, col : col + v.shape[1]] = v.astype(out.dtype)

        fold_piece(put, lambda g, col, k, w=w: w[g * third : (g + 1) * third, col : col + k], cols)


def fin2_kernel(idx, mine, other, gqkv, gout, gvec, ggain, ghid):
    c, core = idx[0], idx[1]
    parts, _, span = mine.shape
    hc = span // 3
    half = gqkv.shape[0] // 2
    width = gout.shape[1]
    piece = gout.shape[0] // parts
    cols = width // 2
    base = half + 16
    tot = mine[0, half:base, :].astype(F32)
    for k in range(1, parts):
        tot = tot + mine[k, half:base, :].astype(F32)
    for n in range(8):
        v = tot[n // 3 : n // 3 + 1, (n % 3) * hc : (n % 3 + 1) * hc]
        if n < 6:
            gvec[n : n + 1, :] = v
        else:
            ggain[n - 6 : n - 5, :] = v
    units = []
    for j in range(parts):
        k = j ^ c
        units.append(mine[k, half:base, :].astype(F32)[2:3, 2 * hc :])
        for src, who in ((mine, core), (other, 1 - core)):
            v = src[k, :half, :].astype(F32)
            for s in range(3):
                gqkv[at(who * half, half, 32), s * width + j * hc : s * width + (j + 1) * hc] = v[
                    :, s * hc : (s + 1) * hc
                ]
            w = src[k, base:, :].astype(F32)
            third = piece // 3
            last = jnp.concatenate([w[:third, cols:], w[third:, cols:]], axis=1)
            for g, v in enumerate((w[:third, :cols], w[third:, :cols], last)):
                row = j * piece + g * third
                gout[row : row + third, at(who * cols, cols, 128)] = v
    ghid[...] = jnp.concatenate(units, axis=1).reshape(ghid.shape)


def call(kernel, out, *args, idx=None, scratch=(), hbm=(), after=(), limit=VMEM_BYTES):
    shapes = [jax.ShapeDtypeStruct(s, d) for s, d in out]
    specs = [
        pl.BlockSpec(memory_space=pltpu.HBM if n in hbm else pltpu.VMEM) for n in range(len(args))
    ]
    args = args + tuple(after)
    specs = specs + [pl.BlockSpec(memory_space=pl.ANY) for _ in after]
    skip = len(args) + (idx is not None)
    drop = len(after)

    def run(*refs):
        kernel(*refs[: skip - drop], *refs[skip:])

    if idx is not None:
        specs = [pl.BlockSpec(memory_space=pltpu.SMEM)] + specs
        args = (idx,) + args
    return pl.pallas_call(
        run if drop else kernel,
        out_shape=shapes,
        in_specs=specs,
        out_specs=[pl.BlockSpec(memory_space=pltpu.VMEM) for _ in shapes],
        scratch_shapes=[pltpu.VMEM(*s) if isinstance(s, tuple) else s for s in scratch],
        compiler_params=pltpu.CompilerParams(vmem_limit_bytes=limit),
        name=kernel.__name__,
        cost_estimate=pl.CostEstimate(flops=COST, bytes_accessed=100000, transcendentals=0),
    )(*args)


def gate(x, after):
    n = len(after)
    return pl.pallas_call(
        lambda *refs: None,
        out_shape=jax.ShapeDtypeStruct(x.shape, x.dtype),
        in_specs=[pl.BlockSpec(memory_space=pl.ANY)] * (n + 1),
        out_specs=pl.BlockSpec(memory_space=pl.ANY),
        input_output_aliases={0: 0},
        compiler_params=pltpu.CompilerParams(vmem_limit_bytes=VMEM_BYTES),
        name="gate_kernel",
    )(x, *after)


def make_body(reps, shards):
    def xor_perm(n, k):
        return [(i, i ^ k) for i in range(n)]

    def swap_core(v):
        return lax.ppermute(v, "rep", xor_perm(reps, 1))

    def swap_part(v, k):
        return lax.ppermute(v, "rep", xor_perm(reps, CORES * k))

    def swap_shard(v, k):
        return lax.ppermute(v, "shard", xor_perm(shards, k))

    def spread_part(v):
        return [v] + [swap_part(v, k) for k in range(1, PARTS)]

    def spread_shard(v):
        return [v] + [swap_shard(v, k) for k in range(1, shards)]

    def relay_shard(v, after=None):
        near, far = swap_shard(v, 1), swap_shard(v, 2)
        if after is not None:
            far = gate(far, after(near))
        return [v, near, far, swap_shard(far, 1)]

    def trade_part(slots):
        return [slots[0]] + [swap_part(slots[k], k) for k in range(1, PARTS)]

    def trade_shard(slots):
        return [slots[0]] + [swap_shard(slots[k], k) for k in range(1, shards)]

    def total(slots):
        acc = slots[0]
        for s in slots[1:]:
            acc = acc + s.astype(F32)
        return acc

    def sum_outer(v):
        step = CORES * PARTS
        while step < reps:
            v = v + lax.ppermute(v, "rep", xor_perm(reps, step))
            step *= 2
        return v

    def body(
        tokens, w_qkv, w_out, w_up, w_down, vec_bias, ln_gain, hidden_bias, seq_lengths, cotangent
    ):
        rows, width = tokens.shape
        hid_own = hidden_bias.shape[0]
        wsh = width // shards
        half = wsh // CORES
        hc = width // PARTS
        fc = hid_own // PARTS
        span = 3 * hc
        piece = wsh // PARTS
        ocol = width // CORES
        rep = lax.axis_index("rep")
        z = lax.axis_index("shard")
        core = rep % CORES
        c = (rep // CORES) % PARTS
        idx = jnp.stack([c, core, z]).astype(jnp.int32)
        mats = [((rows, width), BF)]

        xp, pay1 = call(
            pack_kernel,
            [((rows + 16, width), BF), ((half + 16 + 2 * piece // 3, span), BF)],
            tokens,
            w_qkv,
            w_out,
            vec_bias,
            ln_gain,
            hidden_bias,
            seq_lengths,
            idx=idx,
            hbm=range(7),
            limit=PACK_BYTES,
            scratch=[
                ((half, 3 * width), BF),
                ((piece, ocol), BF),
                (vec_bias.shape, BF),
                (ln_gain.shape, BF),
                ((hid_own,), BF),
                (seq_lengths.shape, jnp.int32),
                pltpu.SemaphoreType.DMA((7,)),
            ],
        )
        xs = spread_part(xp)
        got1 = relay_shard(pay1, lambda near: [xs[3]])
        (pay2,) = call(
            pack2_kernel,
            [((half + fc // CORES, width), BF)],
            w_up,
            w_down,
            idx=idx,
            hbm=(0, 1),
            after=[xp],
            scratch=[((half, w_up.shape[1]), BF), pltpu.SemaphoreType.DMA((2,))],
        )
        pay2 = gate(pay2, [got1[3]] + xs[1:])
        mine1, pay_o = call(
            split_kernel,
            [((shards, half + 16, span), BF), ((shards, piece, ocol), BF)],
            *got1,
        )
        other1 = swap_core(mine1)
        pair_o = jnp.stack([pay_o, swap_part(pay_o, 1)])
        far_o = swap_part(pair_o, 2)

        wq, small, bias = call(
            wq_kernel,
            [((width, span), BF), ((16, width), F32), ((8, span), F32)],
            mine1,
            other1,
            idx=idx,
            after=[pay2],
        )
        att = [
            call(
                attn_kernel,
                [((rows, span), BF), ((HEADS // PARTS, rows, rows), F32), ((rows, hc), BF)],
                x,
                wq,
                bias,
            )
            for k, x in enumerate(xs)
        ]
        mix = trade_part([a[2] for a in att])
        got2 = relay_shard(pay2, lambda near: mix[1:] + [near])
        (mine_o,) = call(
            join_kernel, [((PARTS,) + pay_o.shape, BF)], pair_o, far_o, after=[att[3][2]]
        )
        other_o = swap_core(mine_o)
        (wo,) = call(wo_kernel, [((width, width), BF)], mine_o, other_o, idx=idx)
        y1, y1low, unit1, inv1 = call(
            out_kernel,
            [((rows, width), F32), ((rows, width), BF), ((rows, width), F32), ((rows, 128), F32)],
            tokens,
            *mix,
            wo,
            small,
            idx=idx,
        )
        ys = spread_part(y1low)
        (mine2,) = call(
            stack_kernel, [((shards,) + pay2.shape, BF)], *got2, after=[ys[3]]
        )
        wu, wd = call(
            w2_kernel,
            [((width, shards * fc), BF), ((shards * fc, width), BF)],
            mine2,
            swap_core(mine2),
            idx=idx,
        )
        part_type = [F32] + [BF] * (PARTS - 1)
        ffn = [
            call(
                ffn_kernel,
                [((rows, shards * fc), BF), ((rows, shards * fc), F32), ((rows, width), t)],
                y,
                wu,
                wd,
                small,
            )
            for y, t in zip(ys, part_type)
        ]
        activations, dz, gh2, sm2 = call(
            ln2_kernel,
            mats * 2 + [((rows, width), F32), ((8, width), F32)],
            y1,
            *trade_part([f[2] for f in ffn]),
            small,
            cotangent,
            xp,
        )
        dzs = spread_part(dz)
        ffb = [
            call(
                ffb_kernel, [((rows, shards * fc), BF), ((rows, width), t)], d, wu, wd, f[1]
            )
            for d, f, t in list(zip(dzs, ffn, part_type))[1:]
        ]
        ffb = [
            call(
                ffb_kernel,
                [((rows, shards * fc), BF), ((rows, width), F32)],
                dz,
                wu,
                wd,
                ffn[0][1],
                after=[f[0] for f in ffb],
            )
        ] + ffb
        dyp = trade_part([f[1] for f in ffb])
        rows1 = half + fc // CORES
        give1, keep1, sm3 = call(
            ffw_kernel,
            [((shards, rows1, width), BF)] * 2 + [((8, shards * fc), F32)],
            *[f[0] for f in ffn],
            *dzs,
            *ys,
            *[f[0] for f in ffb],
            idx=idx,
            after=[dyp[3]],
            scratch=[((PARTS * rows, width), BF)] * 2 + [((width, width), BF)],
        )
        def relay_sum(far, send, after):
            got = swap_shard(send, 1)
            (low,) = call(sum_kernel, [(far.shape, BF)], far, got, after=after)
            return low, swap_shard(low, 2)

        def join(own, near, far, after):
            if reps > CORES * PARTS:
                return sum_outer(own + near.astype(F32) + far.astype(F32)).astype(BF)
            return call(sum_kernel, [(own.shape, BF)], own, near, far, after=after)[0]

        def spread_piece(v, after):
            (done,) = call(
                stack_kernel, [((PARTS,) + v.shape, BF)], *spread_part(v), after=after
            )
            return done, swap_core(done)

        def pair_shapes(n, w):
            return [((n, w), F32), ((n, w), BF), ((n, w), F32), ((n, w), BF)]

        own_a, near_a, far_a, send_a = call(
            add_kernel,
            pair_shapes(rows1, width),
            keep1,
            swap_core(give1),
            idx=idx,
            after=[dyp[3]],
        )
        gh1, da, *rest = call(
            ln1b_kernel,
            [((rows, width), F32)] + mats + [((rows, hc), BF)] * PARTS + [((8, width), F32)],
            gh2,
            *dyp,
            unit1,
            inv1,
            small,
            wo,
            idx=idx,
            after=[send_a],
        )
        dm, sm1 = trade_part(rest[:PARTS]), rest[PARTS]
        give_o, keep_o = call(
            outw_kernel,
            [((shards, wsh, ocol), BF)] * 2,
            *mix,
            da,
            idx=idx,
            after=[sm1],
        )
        out_send = call(
            oadd_kernel,
            [((shards, piece, ocol), F32)] + [((shards, piece, ocol), BF)] * 3,
            keep_o,
            swap_core(give_o),
            idx=idx,
        )
        out_got = trade_part(out_send)
        osum = total(out_got)

        dps = [
            call(
                attb_kernel,
                [((rows, span), BF)],
                d,
                a[0],
                a[1],
                after=[out_send[0]] if k < 2 else [],
            )[0]
            for k, (d, a) in enumerate(zip(dm, att))
        ]
        low_a, got_a = relay_sum(far_a, send_a, [dps[3]])
        near_a = swap_shard(gate(near_a, [low_a]), 1)
        rows2 = half + 16
        give2, keep2 = call(
            qw_kernel,
            [((shards, rows2, span), BF)] * 2,
            *xs,
            *dps,
            sm1,
            sm2,
            sm3,
            idx=idx,
            after=[out_got[1], low_a],
            scratch=[
                ((PARTS * rows, width), BF),
                ((PARTS * rows, span), BF),
                ((width, span), BF),
            ],
        )
        dxp = call(
            dx_kernel, [((rows, width), t) for t in part_type], *dps, wq, after=[give2] + out_got[2:]
        )
        dxp_got = trade_part(dxp)
        own_b, near_b, far_b, send_b = call(
            add2_kernel,
            pair_shapes(rows2 + 2 * piece // 3, span),
            keep2,
            swap_core(give2),
            osum,
            idx=idx,
            after=[got_a, near_a, dxp[0]],
        )
        low_b, got_b = relay_sum(far_b, send_b, dxp_got[1:])
        near_b = swap_shard(gate(near_b, [low_b]), 1)
        piece1 = join(own_a, near_a, got_a, [low_b])
        done1 = spread_piece(piece1, [got_b, near_b])
        piece2 = join(own_b, near_b, got_b, [])
        done2 = spread_piece(piece2, [])
        g_tok = gh1 + total(dxp_got)
        gw_up, gw_down, token = call(
            fin1_kernel, [(w_up.shape, F32), (w_down.shape, F32), ((8, 128), F32)], *done1, idx=idx, after=[piece2]
        )
        gw_qkv, gw_out, g_vec, g_gain, g_hidden = call(
            fin2_kernel,
            [
                (w_qkv.shape, F32),
                (w_out.shape, F32),
                ((6, wsh), F32),
                ((2, wsh), F32),
                ((hid_own,), F32),
            ],
            *done2,
            idx=idx,
            after=[token, g_tok],
        )
        return (
            activations,
            g_tok,
            gw_qkv,
            gw_out,
            gw_up,
            gw_down,
            g_vec,
            g_gain,
            g_hidden,
        )

    return body


def solution(mesh):
    body = make_body(mesh.shape["rep"], mesh.shape["shard"])
    both = P(("rep", "shard"), None)
    first = P("shard", None)
    last = P(None, "shard")
    return jax.shard_map(
        body,
        mesh=mesh,
        in_specs=(both, first, first, first, first, last, last, P("shard"), both, both),
        out_specs=(both, both, first, first, first, first, last, last, P("shard")),
        check_vma=False,
    )
```

```python
import functools
import math

import jax
import jax.numpy as jnp
from jax import lax
from jax.experimental import pallas as pl
from jax.experimental.pallas import tpu as pltpu
from jax.sharding import PartitionSpec as P

HEADS = 12
HEAD_DIM = 64
PARTS = 4
CORES = 2
layer_eps = 1e-12
masked_score = -1000000000.0
BF = jnp.bfloat16
F32 = jnp.float32
VMEM_BYTES = 48 * 1024 * 1024
PACK_BYTES = 62 * 1024 * 1024
COST = 11 * 10**9


def mm(a, b):
    return jnp.dot(a, b, preferred_element_type=F32)


def mm_ta(a, b):
    return lax.dot_general(a, b, (((0,), (0,)), ((), ())), preferred_element_type=F32)


def mm_tb(a, b):
    return lax.dot_general(a, b, (((1,), (1,)), ((), ())), preferred_element_type=F32)


def at(start, size, unit):
    return pl.ds(pl.multiple_of(start, unit), size)


def norm_stats(h):
    centre = h - jnp.mean(h, axis=-1, keepdims=True)
    inv = lax.rsqrt(jnp.mean(centre * centre, axis=-1, keepdims=True) + layer_eps)
    return centre * inv, inv


def norm_back(g, unit, inv, gain):
    gg = g * gain
    m1 = jnp.mean(gg, axis=-1, keepdims=True)
    m2 = jnp.mean(gg * unit, axis=-1, keepdims=True)
    return inv * (gg - m1 - unit * m2)


def gelu_parts(u):
    phi = 0.5 * (1.0 + lax.erf(u * (1.0 / math.sqrt(2.0))))
    dens = jnp.exp(-0.5 * u * u) * (1.0 / math.sqrt(2.0 * math.pi))
    return phi, phi + u * dens


def col_sum(v):
    return jnp.sum(v, axis=0, keepdims=True)


def fold_piece(put, get, cols):
    put(0, 0, get(0, 0, cols))
    put(1, 0, get(1, 0, cols))
    put(0, cols, get(2, 0, cols // 2))
    put(1, cols, get(2, cols // 2, cols // 2))


def pack_kernel(idx, tok, wqkv, wout, vec_in, gain_in, hid_in, lens_in, xp, pay, bq, bo, vec, gain, hid, lens, sem):
    rows, width = tok.shape
    half = bq.shape[0]
    piece, ocol = bo.shape
    hc = width // PARTS
    fc = hid.shape[0] // PARTS
    load_q = pltpu.make_async_copy(wqkv.at[at(idx[1] * half, half, 32)], bq, sem.at[0])
    load_o = pltpu.make_async_copy(
        wout.at[at(idx[0] * piece, piece, 16), at(idx[1] * ocol, ocol, 128)], bo, sem.at[1]
    )
    load_x = pltpu.make_async_copy(tok, xp.at[:rows], sem.at[2])
    small = [
        pltpu.make_async_copy(a, b, sem.at[3 + n])
        for n, (a, b) in enumerate(
            ((vec_in, vec), (gain_in, gain), (hid_in, hid), (lens_in, lens))
        )
    ]
    load_q.start()
    load_x.start()
    load_o.start()
    for load in small:
        load.start()
    base = half + 16
    pay[half:base] = jnp.zeros((16, 3 * hc), BF)
    xp[rows:] = jnp.zeros((16, width), BF)
    for load in small:
        load.wait()
    xp[rows : rows + 1, : lens.shape[1]] = lens[...].astype(BF)
    for n in range(8):
        src = vec[n : n + 1, :] if n < 6 else gain[n - 6 : n - 5, :]
        pay[half + n // 3 : half + n // 3 + 1, (n % 3) * hc : (n % 3 + 1) * hc] = src
    load_o.wait()
    third = piece // 3

    def put(row, col, v):
        pay[base + row * third : base + (row + 1) * third, col : col + v.shape[1]] = v

    fold_piece(put, lambda g, col, n: bo[g * third : (g + 1) * third, col : col + n], ocol)
    load_q.wait()
    units = hid[...].reshape(1, hid.shape[0])
    for j in range(PARTS):

        @pl.when(idx[0] == j)
        def _(j=j):
            pay[half + 2 : half + 3, 2 * hc :] = units[:, j * fc : (j + 1) * fc]
            for s in range(3):
                pay[:half, s * hc : (s + 1) * hc] = bq[
                    :, s * width + j * hc : s * width + (j + 1) * hc
                ]

    load_x.wait()


def pack2_kernel(idx, wup, wdown, pay, bu, sem):
    half = bu.shape[0]
    fc = pay.shape[0] - half
    units = wdown.shape[0]
    shards = wup.shape[1] // units
    fpart = units // PARTS
    load_u = pltpu.make_async_copy(wup.at[at(idx[1] * half, half, 32)], bu, sem.at[0])
    load_d = pltpu.make_async_copy(
        wdown.at[at(idx[0] * fpart + idx[1] * fc, fc, 32)], pay.at[half:], sem.at[1]
    )
    load_u.start()
    load_d.start()
    load_u.wait()
    for j in range(PARTS):

        @pl.when(idx[0] == j)
        def _(j=j):
            for s in range(shards):
                base = (s * PARTS + j) * fpart
                pay[:half, s * fpart : (s + 1) * fpart] = bu[:, base : base + fpart]

    load_d.wait()


def split_kernel(g0, g1, g2, g3, first, second):
    base = first.shape[1]
    cols = second.shape[2]
    third = second.shape[1] // 3
    for k, g in enumerate((g0, g1, g2, g3)):
        first[k] = g[:base, :]
        top, low = g[base : base + third, :], g[base + third :, :]
        second[k, :third] = top[:, :cols]
        second[k, third : 2 * third] = low[:, :cols]
        second[k, 2 * third :, : cols // 2] = top[:, cols:]
        second[k, 2 * third :, cols // 2 :] = low[:, cols:]


def sum_kernel(*refs):
    out = refs[-1]
    v = refs[0][...].astype(F32)
    for r in refs[1:-1]:
        v = v + r[...].astype(F32)
    out[...] = v.astype(out.dtype)


def wq_kernel(idx, mine, other, wq, small, bias):
    c, core, z = idx[0], idx[1], idx[2]
    shards, _, span = mine.shape
    hc = span // 3
    half = wq.shape[0] // shards // CORES
    for m in range(shards):
        base = (z ^ m) * (CORES * half)
        wq[at(base + core * half, half, 32), :] = mine[m, :half, :]
        wq[at(base + (1 - core) * half, half, 32), :] = other[m, :half, :]
    small[...] = jnp.zeros_like(small)
    for j in range(shards):
        e = mine[j ^ z, half:, :].astype(F32)
        for n in range(9):
            small[n : n + 1, j * hc : (j + 1) * hc] = e[
                n // 3 : n // 3 + 1, (n % 3) * hc : (n % 3 + 1) * hc
            ]
    e = mine[c ^ z, half:, :].astype(F32)[:1]
    row = jnp.concatenate([e[:, :hc], jnp.zeros((1, hc), F32), e[:, hc : 2 * hc]], axis=1)
    bias[...] = jnp.broadcast_to(row, bias.shape)


def attn_kernel(x, wq, bias, pj, probs, out):
    rows, span = pj.shape
    hc = span // 3
    heads = hc // HEAD_DIM
    scale = 1.0 / math.sqrt(HEAD_DIM)
    pj[...] = (mm(x[:rows, :], wq[...]) + bias[:1, :]).astype(BF)
    pos_r = lax.broadcasted_iota(jnp.int32, (rows, 1), 0).astype(F32)
    pos_c = lax.broadcasted_iota(jnp.int32, (1, rows), 1).astype(F32)
    lens = x[rows : rows + 16, :128].astype(F32)[:1]
    end = jnp.zeros((1, 1), F32)
    seg_r = jnp.zeros((rows, 1), F32)
    seg_c = jnp.zeros((1, rows), F32)
    for n in range(3):
        end = end + lens[:, n : n + 1]
        seg_r = seg_r + (pos_r >= end).astype(F32)
        seg_c = seg_c + (pos_c >= end).astype(F32)
    same = seg_r == seg_c
    pb = pj[...]
    mixes = []
    for h in range(heads):
        q = pb[:, h * HEAD_DIM : (h + 1) * HEAD_DIM]
        k = pb[:, hc + h * HEAD_DIM : hc + (h + 1) * HEAD_DIM]
        v = pb[:, 2 * hc + h * HEAD_DIM : 2 * hc + (h + 1) * HEAD_DIM]
        s = jnp.where(same, mm_tb(q, k) * scale, masked_score)
        e = jnp.exp(s - jnp.max(s, axis=-1, keepdims=True))
        p = e / jnp.sum(e, axis=-1, keepdims=True)
        probs[h] = p
        mixes.append(mm(p.astype(BF), v))
    out[...] = jnp.concatenate(mixes, axis=1).astype(BF)


def wo_kernel(idx, mine, other, wo):
    c, core, z = idx[0], idx[1], idx[2]
    parts, shards, piece, cols = mine.shape
    for k in range(parts):
        for m in range(shards):
            base = at((z ^ m) * (parts * piece) + (c ^ k) * piece, piece, 16)
            wo[base, at(core * cols, cols, 128)] = mine[k, m]
            wo[base, at((1 - core) * cols, cols, 128)] = other[k, m]


def out_kernel(idx, tok, m0, m1, m2, m3, wo, small, y1, y1low, unit, inv):
    c = idx[0]
    hc = m0.shape[1]
    acc = small[2:3, :]
    for k, m in enumerate((m0, m1, m2, m3)):
        acc = acc + mm(m[...], wo[at((c ^ k) * hc, hc, 64), :])
    u, r = norm_stats(tok[...].astype(F32) + acc)
    unit[...] = u
    inv[...] = jnp.broadcast_to(r, inv.shape)
    y = u * small[6:7, :] + small[3:4, :]
    y1[...] = y
    y1low[...] = y.astype(BF)


def join_kernel(near, far, out):
    out[:2] = near[...]
    out[2:] = far[...]


def stack_kernel(g0, g1, g2, g3, out):
    for k, g in enumerate((g0, g1, g2, g3)):
        out[k] = g[...]


def w2_kernel(idx, mine, other, wu, wd):
    core, z = idx[1], idx[2]
    half = mine.shape[1] // 2
    for m in range(mine.shape[0]):
        base = (z ^ m) * (2 * half)
        lo = at(base + core * half, half, 32)
        hi = at(base + (1 - core) * half, half, 32)
        wu[lo, :] = mine[m, :half, :]
        wu[hi, :] = other[m, :half, :]
        wd[lo, :] = mine[m, half:, :]
        wd[hi, :] = other[m, half:, :]


def ffn_kernel(y, wu, wd, small, act, slope, out):
    u = mm(y[...], wu[...]) + small[8:9, :]
    phi, slp = gelu_parts(u)
    a = (u * phi).astype(BF)
    act[...] = a
    slope[...] = slp
    out[...] = mm(a, wd[...]).astype(out.dtype)


def ln2_kernel(y1, z0, r1, r2, r3, small, cot, x0, actv, dz, gh2, sm):
    rows = y1.shape[0]
    branch = z0[...] + r1[...].astype(F32) + r2[...].astype(F32) + r3[...].astype(F32)
    u, r = norm_stats(y1[...] + (branch + small[4:5, :]))
    lens = x0[rows : rows + 16, :128].astype(F32)[:1]
    total = lens[:, 0:1] + lens[:, 1:2] + lens[:, 2:3]
    keep = (lax.broadcasted_iota(jnp.int32, (rows, 1), 0).astype(F32) < total).astype(F32)
    actv[...] = ((u * small[7:8, :] + small[5:6, :]) * keep).astype(BF)
    g = cot[...].astype(F32) * keep
    gh = norm_back(g, u, r, small[7:8, :])
    gh2[...] = gh
    low = gh.astype(BF)
    dz[...] = low
    sm[...] = jnp.zeros_like(sm)
    sm[0:1, :] = col_sum(low.astype(F32))
    sm[1:2, :] = col_sum(g)
    sm[2:3, :] = col_sum(g * u)


def ffb_kernel(d, wu, wd, slope, du, out):
    t = (mm_tb(d[...], wd[...]) * slope[...]).astype(BF)
    du[...] = t
    out[...] = mm_tb(t, wu[...]).astype(out.dtype)


def ffw_kernel(idx, *refs):
    core = idx[1]
    groups = [refs[n * PARTS : (n + 1) * PARTS] for n in range(4)]
    give, mine, hid, left, right, full = refs[4 * PARTS :]
    rows, width = groups[0][0].shape
    shards = give.shape[0]
    half = width // shards // CORES
    acts, dzs, ys, dus = groups
    h = None
    for base, lefts, rights in ((0, ys, dus), (half, acts, dzs)):
        for k in range(PARTS):
            left[k * rows : (k + 1) * rows, :] = lefts[k][...]
            right[k * rows : (k + 1) * rows, :] = rights[k][...]
        if base == 0:
            h = col_sum(right[...].astype(F32))
        full[...] = mm_ta(left[...], right[...]).astype(BF)
        for j in range(shards):
            mine[j, base : base + half, :] = full[at(j * 2 * half + core * half, half, 32), :]
            give[j, base : base + half, :] = full[
                at(j * 2 * half + (1 - core) * half, half, 32), :
            ]
    hid[...] = jnp.broadcast_to(h, hid.shape)


def add_kernel(idx, mine, got, own, near, far, send):
    z = idx[2]
    for k, out in enumerate((own, near, far, send)):
        out[...] = (mine[z ^ k].astype(F32) + got[z ^ k].astype(F32)).astype(out.dtype)


def fin1_kernel(idx, mine, other, gup, gdown, token):
    c, core = idx[0], idx[1]
    parts, _, width = mine.shape
    half = gup.shape[0] // 2
    fc = gdown.shape[0] // parts
    shards = gup.shape[1] // (parts * fc)
    for j in range(parts):
        k = j ^ c
        token[...] = jnp.zeros_like(token)
        for src, row in ((mine, core * half), (other, (1 - core) * half)):
            v = src[k, :half, :].astype(F32)
            for s in range(shards):
                base = (s * parts + j) * fc
                gup[at(row, half, 32), base : base + fc] = v[:, s * fc : (s + 1) * fc]
            gdown[at(j * fc + row, half, 32), :] = src[k, half : 2 * half, :].astype(F32)


def ln1b_kernel(idx, gh2, o0, r1, r2, r3, unit, inv, small, wo, gh1, da, m0, m1, m2, m3, sm):
    c = idx[0]
    hc = m0.shape[1]
    dy = gh2[...] + o0[...] + r1[...].astype(F32) + r2[...].astype(F32) + r3[...].astype(F32)
    u = unit[...]
    gh = norm_back(dy, u, inv[:, :1], small[6:7, :])
    gh1[...] = gh
    low = gh.astype(BF)
    da[...] = low
    for k, m in enumerate((m0, m1, m2, m3)):
        m[...] = mm_tb(low, wo[at((c ^ k) * hc, hc, 64), :]).astype(BF)
    sm[...] = jnp.zeros_like(sm)
    sm[0:1, :] = col_sum(low.astype(F32))
    sm[1:2, :] = col_sum(dy)
    sm[2:3, :] = col_sum(dy * u)


def outw_kernel(idx, m0, m1, m2, m3, da, give, mine):
    c, core = idx[0], idx[1]
    cols = give.shape[2]
    lo, hi = da[:, :cols], da[:, cols:]
    first = core == 0
    keep = jnp.where(first, lo.astype(F32), hi.astype(F32)).astype(BF)
    pass_on = jnp.where(first, hi.astype(F32), lo.astype(F32)).astype(BF)
    for k, m in enumerate((m0, m1, m2, m3)):
        mine[c ^ k] = mm_ta(m[...], keep).astype(BF)
        give[c ^ k] = mm_ta(m[...], pass_on).astype(BF)


def oadd_kernel(idx, mine, got, own, s1, s2, s3):
    c = idx[0]
    shards, piece = own.shape[0], own.shape[1]
    for k, out in enumerate((own, s1, s2, s3)):
        rng = at((c ^ k) * piece, piece, 16)
        for j in range(shards):
            v = mine[j, rng, :].astype(F32) + got[j, rng, :].astype(F32)
            out[j] = v.astype(out.dtype)


def attb_kernel(d, pj, probs, dp):
    rows, hc = d.shape
    heads = hc // HEAD_DIM
    scale = 1.0 / math.sqrt(HEAD_DIM)
    pb = pj[...]
    db = d[...]
    dqs, dks, dvs = [], [], []
    for h in range(heads):
        q = pb[:, h * HEAD_DIM : (h + 1) * HEAD_DIM]
        k = pb[:, hc + h * HEAD_DIM : hc + (h + 1) * HEAD_DIM]
        v = pb[:, 2 * hc + h * HEAD_DIM : 2 * hc + (h + 1) * HEAD_DIM]
        g = db[:, h * HEAD_DIM : (h + 1) * HEAD_DIM]
        p = probs[h]
        dvs.append(mm_ta(p.astype(BF), g))
        dpr = mm_tb(g, v)
        inner = jnp.sum(p * dpr, axis=-1, keepdims=True)
        ds = (p * (dpr - inner)).astype(BF)
        dqs.append(mm(ds, k) * scale)
        dks.append(mm_ta(ds, q) * scale)
    dp[...] = jnp.concatenate(dqs + dks + dvs, axis=1).astype(BF)


def dx_kernel(d0, d1, d2, d3, wq, o0, o1, o2, o3):
    for d, out in ((d0, o0), (d1, o1), (d2, o2), (d3, o3)):
        out[...] = mm_tb(d[...], wq[...]).astype(out.dtype)


def qw_kernel(idx, x0, x1, x2, x3, d0, d1, d2, d3, sm1, sm2, hid, give, mine, xg, dp, full):
    c, core = idx[0], idx[1]
    shards, _, span = give.shape
    rows = d0.shape[0]
    hc = span // 3
    half = xg.shape[1] // shards // CORES
    for k, (x, d) in enumerate(((x0, d0), (x1, d1), (x2, d2), (x3, d3))):
        xg[k * rows : (k + 1) * rows, :] = x[:rows, :]
        dp[k * rows : (k + 1) * rows, :] = d[...]
    full[...] = mm_ta(xg[...], dp[...]).astype(BF)
    cols = col_sum(dp[...].astype(F32))
    vecs = (sm1[0:1], sm1[1:2], sm2[0:1], sm2[1:2], sm1[2:3], sm2[2:3])
    for j in range(shards):
        mine[j, :half, :] = full[at(j * 2 * half + core * half, half, 32), :]
        give[j, :half, :] = full[at(j * 2 * half + (1 - core) * half, half, 32), :]
        part = [v[:, j * hc : (j + 1) * hc] for v in vecs]
        own = jnp.where(c == j, 1.0, 0.0)
        rows = jnp.concatenate(
            [
                jnp.concatenate([cols[:, :hc] * own, cols[:, 2 * hc :] * own, part[0]], axis=1),
                jnp.concatenate(part[1:4], axis=1),
                jnp.concatenate(part[4:6] + [hid[:1, j * hc : (j + 1) * hc]], axis=1),
                jnp.zeros((13, span), F32),
            ],
            axis=0,
        ).astype(BF)
        mine[j, half:, :] = rows
        give[j, half:, :] = rows


def add2_kernel(idx, mine, got, osum, own, near, far, send):
    z = idx[2]
    base, _ = mine.shape[1:]
    piece, cols = osum.shape[1:]
    third = piece // 3
    for n, out in enumerate((own, near, far, send)):
        j = z ^ n
        out[:base, :] = (mine[j].astype(F32) + got[j].astype(F32)).astype(out.dtype)
        w = osum[j]

        def put(row, col, v, out=out):
            rng = slice(base + row * third, base + (row + 1) * third)
            out[rng, col : col + v.shape[1]] = v.astype(out.dtype)

        fold_piece(put, lambda g, col, k, w=w: w[g * third : (g + 1) * third, col : col + k], cols)


def fin2_kernel(idx, mine, other, gqkv, gout, gvec, ggain, ghid):
    c, core = idx[0], idx[1]
    parts, _, span = mine.shape
    hc = span // 3
    half = gqkv.shape[0] // 2
    width = gout.shape[1]
    piece = gout.shape[0] // parts
    cols = width // 2
    base = half + 16
    tot = mine[0, half:base, :].astype(F32)
    for k in range(1, parts):
        tot = tot + mine[k, half:base, :].astype(F32)
    for n in range(8):
        v = tot[n // 3 : n // 3 + 1, (n % 3) * hc : (n % 3 + 1) * hc]
        if n < 6:
            gvec[n : n + 1, :] = v
        else:
            ggain[n - 6 : n - 5, :] = v
    units = []
    for j in range(parts):
        k = j ^ c
        units.append(mine[k, half:base, :].astype(F32)[2:3, 2 * hc :])
        for src, who in ((mine, core), (other, 1 - core)):
            v = src[k, :half, :].astype(F32)
            for s in range(3):
                gqkv[at(who * half, half, 32), s * width + j * hc : s * width + (j + 1) * hc] = v[
                    :, s * hc : (s + 1) * hc
                ]
            w = src[k, base:, :].astype(F32)
            third = piece // 3
            last = jnp.concatenate([w[:third, cols:], w[third:, cols:]], axis=1)
            for g, v in enumerate((w[:third, :cols], w[third:, :cols], last)):
                row = j * piece + g * third
                gout[row : row + third, at(who * cols, cols, 128)] = v
    ghid[...] = jnp.concatenate(units, axis=1).reshape(ghid.shape)


def call(kernel, out, *args, idx=None, scratch=(), hbm=(), after=(), limit=VMEM_BYTES):
    shapes = [jax.ShapeDtypeStruct(s, d) for s, d in out]
    specs = [
        pl.BlockSpec(memory_space=pltpu.HBM if n in hbm else pltpu.VMEM) for n in range(len(args))
    ]
    args = args + tuple(after)
    specs = specs + [pl.BlockSpec(memory_space=pl.ANY) for _ in after]
    skip = len(args) + (idx is not None)
    drop = len(after)

    def run(*refs):
        kernel(*refs[: skip - drop], *refs[skip:])

    if idx is not None:
        specs = [pl.BlockSpec(memory_space=pltpu.SMEM)] + specs
        args = (idx,) + args
    return pl.pallas_call(
        run if drop else kernel,
        out_shape=shapes,
        in_specs=specs,
        out_specs=[pl.BlockSpec(memory_space=pltpu.VMEM) for _ in shapes],
        scratch_shapes=[pltpu.VMEM(*s) if isinstance(s, tuple) else s for s in scratch],
        compiler_params=pltpu.CompilerParams(vmem_limit_bytes=limit),
        name=kernel.__name__,
        cost_estimate=pl.CostEstimate(flops=COST, bytes_accessed=100000, transcendentals=0),
    )(*args)


def gate(x, after):
    n = len(after)
    return pl.pallas_call(
        lambda *refs: None,
        out_shape=jax.ShapeDtypeStruct(x.shape, x.dtype),
        in_specs=[pl.BlockSpec(memory_space=pl.ANY)] * (n + 1),
        out_specs=pl.BlockSpec(memory_space=pl.ANY),
        input_output_aliases={0: 0},
        compiler_params=pltpu.CompilerParams(vmem_limit_bytes=VMEM_BYTES),
        name="gate_kernel",
    )(x, *after)


def make_body(reps, shards):
    def xor_perm(n, k):
        return [(i, i ^ k) for i in range(n)]

    def swap_core(v):
        return lax.ppermute(v, "rep", xor_perm(reps, 1))

    def swap_part(v, k):
        return lax.ppermute(v, "rep", xor_perm(reps, CORES * k))

    def swap_shard(v, k):
        return lax.ppermute(v, "shard", xor_perm(shards, k))

    def spread_part(v):
        return [v] + [swap_part(v, k) for k in range(1, PARTS)]

    def spread_shard(v):
        return [v] + [swap_shard(v, k) for k in range(1, shards)]

    def relay_shard(v, after=None):
        near, far = swap_shard(v, 1), swap_shard(v, 2)
        if after is not None:
            far = gate(far, after(near))
        return [v, near, far, swap_shard(far, 1)]

    def trade_part(slots):
        return [slots[0]] + [swap_part(slots[k], k) for k in range(1, PARTS)]

    def trade_shard(slots):
        return [slots[0]] + [swap_shard(slots[k], k) for k in range(1, shards)]

    def total(slots):
        acc = slots[0]
        for s in slots[1:]:
            acc = acc + s.astype(F32)
        return acc

    def sum_outer(v):
        step = CORES * PARTS
        while step < reps:
            v = v + lax.ppermute(v, "rep", xor_perm(reps, step))
            step *= 2
        return v

    def body(
        tokens, w_qkv, w_out, w_up, w_down, vec_bias, ln_gain, hidden_bias, seq_lengths, cotangent
    ):
        rows, width = tokens.shape
        hid_own = hidden_bias.shape[0]
        wsh = width // shards
        half = wsh // CORES
        hc = width // PARTS
        fc = hid_own // PARTS
        span = 3 * hc
        piece = wsh // PARTS
        ocol = width // CORES
        rep = lax.axis_index("rep")
        z = lax.axis_index("shard")
        core = rep % CORES
        c = (rep // CORES) % PARTS
        idx = jnp.stack([c, core, z]).astype(jnp.int32)
        mats = [((rows, width), BF)]

        xp, pay1 = call(
            pack_kernel,
            [((rows + 16, width), BF), ((half + 16 + 2 * piece // 3, span), BF)],
            tokens,
            w_qkv,
            w_out,
            vec_bias,
            ln_gain,
            hidden_bias,
            seq_lengths,
            idx=idx,
            hbm=range(7),
            limit=PACK_BYTES,
            scratch=[
                ((half, 3 * width), BF),
                ((piece, ocol), BF),
                (vec_bias.shape, BF),
                (ln_gain.shape, BF),
                ((hid_own,), BF),
                (seq_lengths.shape, jnp.int32),
                pltpu.SemaphoreType.DMA((7,)),
            ],
        )
        xs = spread_part(xp)
        got1 = relay_shard(pay1, lambda near: [xs[3]])
        (pay2,) = call(
            pack2_kernel,
            [((half + fc // CORES, width), BF)],
            w_up,
            w_down,
            idx=idx,
            hbm=(0, 1),
            after=[xp],
            scratch=[((half, w_up.shape[1]), BF), pltpu.SemaphoreType.DMA((2,))],
        )
        pay2 = gate(pay2, [got1[3]] + xs[1:])
        mine1, pay_o = call(
            split_kernel,
            [((shards, half + 16, span), BF), ((shards, piece, ocol), BF)],
            *got1,
        )
        other1 = swap_core(mine1)
        pair_o = jnp.stack([pay_o, swap_part(pay_o, 1)])
        far_o = swap_part(pair_o, 2)

        wq, small, bias = call(
            wq_kernel,
            [((width, span), BF), ((16, width), F32), ((8, span), F32)],
            mine1,
            other1,
            idx=idx,
            after=[pay2],
        )
        att = [
            call(
                attn_kernel,
                [((rows, span), BF), ((HEADS // PARTS, rows, rows), F32), ((rows, hc), BF)],
                x,
                wq,
                bias,
            )
            for k, x in enumerate(xs)
        ]
        mix = trade_part([a[2] for a in att])
        got2 = relay_shard(pay2, lambda near: mix[1:] + [near])
        (mine_o,) = call(
            join_kernel, [((PARTS,) + pay_o.shape, BF)], pair_o, far_o, after=[att[3][2]]
        )
        other_o = swap_core(mine_o)
        (wo,) = call(wo_kernel, [((width, width), BF)], mine_o, other_o, idx=idx)
        y1, y1low, unit1, inv1 = call(
            out_kernel,
            [((rows, width), F32), ((rows, width), BF), ((rows, width), F32), ((rows, 128), F32)],
            tokens,
            *mix,
            wo,
            small,
            idx=idx,
        )
        ys = spread_part(y1low)
        (mine2,) = call(
            stack_kernel, [((shards,) + pay2.shape, BF)], *got2, after=[ys[3]]
        )
        wu, wd = call(
            w2_kernel,
            [((width, shards * fc), BF), ((shards * fc, width), BF)],
            mine2,
            swap_core(mine2),
            idx=idx,
        )
        part_type = [F32] + [BF] * (PARTS - 1)
        ffn = [
            call(
                ffn_kernel,
                [((rows, shards * fc), BF), ((rows, shards * fc), F32), ((rows, width), t)],
                y,
                wu,
                wd,
                small,
            )
            for y, t in zip(ys, part_type)
        ]
        activations, dz, gh2, sm2 = call(
            ln2_kernel,
            mats * 2 + [((rows, width), F32), ((8, width), F32)],
            y1,
            *trade_part([f[2] for f in ffn]),
            small,
            cotangent,
            xp,
        )
        dzs = spread_part(dz)
        ffb = [
            call(
                ffb_kernel, [((rows, shards * fc), BF), ((rows, width), t)], d, wu, wd, f[1]
            )
            for d, f, t in list(zip(dzs, ffn, part_type))[1:]
        ]
        ffb = [
            call(
                ffb_kernel,
                [((rows, shards * fc), BF), ((rows, width), F32)],
                dz,
                wu,
                wd,
                ffn[0][1],
                after=[f[0] for f in ffb],
            )
        ] + ffb
        dyp = trade_part([f[1] for f in ffb])
        rows1 = half + fc // CORES
        give1, keep1, sm3 = call(
            ffw_kernel,
            [((shards, rows1, width), BF)] * 2 + [((8, shards * fc), F32)],
            *[f[0] for f in ffn],
            *dzs,
            *ys,
            *[f[0] for f in ffb],
            idx=idx,
            after=[dyp[3]],
            scratch=[((PARTS * rows, width), BF)] * 2 + [((width, width), BF)],
        )
        def relay_sum(far, send, after):
            got = swap_shard(send, 1)
            (low,) = call(sum_kernel, [(far.shape, BF)], far, got, after=after)
            return low, swap_shard(low, 2)

        def join(own, near, far, after):
            if reps > CORES * PARTS:
                return sum_outer(own + near.astype(F32) + far.astype(F32)).astype(BF)
            return call(sum_kernel, [(own.shape, BF)], own, near, far, after=after)[0]

        def spread_piece(v, after):
            (done,) = call(
                stack_kernel, [((PARTS,) + v.shape, BF)], *spread_part(v), after=after
            )
            return done, swap_core(done)

        def pair_shapes(n, w):
            return [((n, w), F32), ((n, w), BF), ((n, w), F32), ((n, w), BF)]

        own_a, near_a, far_a, send_a = call(
            add_kernel,
            pair_shapes(rows1, width),
            keep1,
            swap_core(give1),
            idx=idx,
            after=[dyp[3]],
        )
        gh1, da, *rest = call(
            ln1b_kernel,
            [((rows, width), F32)] + mats + [((rows, hc), BF)] * PARTS + [((8, width), F32)],
            gh2,
            *dyp,
            unit1,
            inv1,
            small,
            wo,
            idx=idx,
            after=[send_a],
        )
        dm, sm1 = trade_part(rest[:PARTS]), rest[PARTS]
        give_o, keep_o = call(
            outw_kernel,
            [((shards, wsh, ocol), BF)] * 2,
            *mix,
            da,
            idx=idx,
            after=[sm1],
        )
        out_send = call(
            oadd_kernel,
            [((shards, piece, ocol), F32)] + [((shards, piece, ocol), BF)] * 3,
            keep_o,
            swap_core(give_o),
            idx=idx,
        )
        out_got = trade_part(out_send)
        osum = total(out_got)

        dps = [
            call(
                attb_kernel,
                [((rows, span), BF)],
                d,
                a[0],
                a[1],
                after=[out_send[0]] if k < 2 else [],
            )[0]
            for k, (d, a) in enumerate(zip(dm, att))
        ]
        low_a, got_a = relay_sum(far_a, send_a, [dps[3]])
        near_a = swap_shard(gate(near_a, [low_a]), 1)
        rows2 = half + 16
        give2, keep2 = call(
            qw_kernel,
            [((shards, rows2, span), BF)] * 2,
            *xs,
            *dps,
            sm1,
            sm2,
            sm3,
            idx=idx,
            after=[out_got[1], low_a],
            scratch=[
                ((PARTS * rows, width), BF),
                ((PARTS * rows, span), BF),
                ((width, span), BF),
            ],
        )
        dxp = call(
            dx_kernel, [((rows, width), t) for t in part_type], *dps, wq, after=[give2] + out_got[2:]
        )
        dxp_got = trade_part(dxp)
        own_b, near_b, far_b, send_b = call(
            add2_kernel,
            pair_shapes(rows2 + 2 * piece // 3, span),
            keep2,
            swap_core(give2),
            osum,
            idx=idx,
            after=[got_a, near_a, dxp[0]],
        )
        low_b, got_b = relay_sum(far_b, send_b, [dxp_got[3]])
        near_b = swap_shard(gate(near_b, [low_b]), 1)
        piece1 = join(own_a, near_a, got_a, [low_b])
        done1 = spread_piece(piece1, [got_b, near_b])
        piece2 = join(own_b, near_b, got_b, [])
        done2 = spread_piece(piece2, [])
        g_tok = gh1 + total(dxp_got)
        gw_up, gw_down, token = call(
            fin1_kernel, [(w_up.shape, F32), (w_down.shape, F32), ((8, 128), F32)], *done1, idx=idx, after=[piece2]
        )
        gw_qkv, gw_out, g_vec, g_gain, g_hidden = call(
            fin2_kernel,
            [
                (w_qkv.shape, F32),
                (w_out.shape, F32),
                ((6, wsh), F32),
                ((2, wsh), F32),
                ((hid_own,), F32),
            ],
            *done2,
            idx=idx,
            after=[token, g_tok],
        )
        return (
            activations,
            g_tok,
            gw_qkv,
            gw_out,
            gw_up,
            gw_down,
            g_vec,
            g_gain,
            g_hidden,
        )

    return body


def solution(mesh):
    body = make_body(mesh.shape["rep"], mesh.shape["shard"])
    both = P(("rep", "shard"), None)
    first = P("shard", None)
    last = P(None, "shard")
    return jax.shard_map(
        body,
        mesh=mesh,
        in_specs=(both, first, first, first, first, last, last, P("shard"), both, both),
        out_specs=(both, both, first, first, first, first, last, last, P("shard")),
        check_vma=False,
    )
```
